32 devices in a mesh: dp: 2 (over core), seq: 4 (over y, x), tensor: 4 (over z).
Axes of the slice: x: 2, y: 2, z: 4, core: 2. Of those that a mesh axis runs over, the one named last changes fastest.
Arguments:
- inputs: bfloat16 [2, 8192, 2304], P('dp', 'seq'), may hold values from -40 to 40
- positions: int32 [2, 8192], P('dp', 'seq'), may hold values from 0 to 7679, as said below
- query_weight: bfloat16 [2304, 2048], P(('dp', 'seq'), 'tensor'), may hold values from -0.21875 to 0.21875
- key_weight: bfloat16 [2304, 1024], P(('dp', 'seq'), 'tensor'), may hold values from -0.21875 to 0.21875
- value_weight: bfloat16 [2304, 1024], P(('dp', 'seq'), 'tensor'), may hold values from -0.125 to 0.125
- output_weight: bfloat16 [2304, 2048], P(('dp', 'seq'), 'tensor'), may hold values from -4 to 4
- gate_weight: bfloat16 [2304, 9216], P(('dp', 'seq'), 'tensor'), may hold values from -0.125 to 0.125
- up_weight: bfloat16 [2304, 9216], P(('dp', 'seq'), 'tensor'), may hold values from -0.125 to 0.125
- down_weight: bfloat16 [2304, 9216], P(('dp', 'seq'), 'tensor'), may hold values from -0.0625 to 0.0625
- pre_attention: bfloat16 [2304], P(('dp', 'seq')), may hold values from -0.59765625 to 0.59765625
- post_attention: bfloat16 [2304], P(('dp', 'seq')), may hold values from -0.59765625 to 0.59765625
- pre_feedforward: bfloat16 [2304], P(('dp', 'seq')), may hold values from -0.59765625 to 0.59765625
- post_feedforward: bfloat16 [2304], P(('dp', 'seq')), may hold values from -0.59765625 to 0.59765625
- cotangent: bfloat16 [2, 8192, 2304], P('dp', 'seq'), may hold values from -6 to 6
Outputs:
- layer_output: bfloat16 [2, 8192, 2304], P('dp', 'seq')
- input_gradient: float32 [2, 8192, 2304], P('dp', 'seq')
- query_gradient: float32 [2304, 2048], P(('dp', 'seq'), 'tensor')
- key_gradient: float32 [2304, 1024], P(('dp', 'seq'), 'tensor')
- value_gradient: float32 [2304, 1024], P(('dp', 'seq'), 'tensor')
- output_gradient: float32 [2304, 2048], P(('dp', 'seq'), 'tensor')
- gate_gradient: float32 [2304, 9216], P(('dp', 'seq'), 'tensor')
- up_gradient: float32 [2304, 9216], P(('dp', 'seq'), 'tensor')
- down_gradient: float32 [2304, 9216], P(('dp', 'seq'), 'tensor')
- pre_attention_gradient: float32 [2304], P(('dp', 'seq'))
- post_attention_gradient: float32 [2304], P(('dp', 'seq'))
- pre_feedforward_gradient: float32 [2304], P(('dp', 'seq'))
- post_feedforward_gradient: float32 [2304], P(('dp', 'seq'))
The draws below stay inside these ranges and needn't reach their ends.
Inputs may be any that keep to these rules, and one draw needn't show every extreme that they name: `positions`: each row packs documents: a token's position is its index within its document, rising by one from token to token and starting again at 0 where a document begins. Every row holds one main document that begins within the row's first 2048 tokens (at token 0 in the first row) and ends at token 7679, with at most two documents before it and one document of 512 tokens after it.
All inputs are finite; a program needn't handle non-finite values.
Results may differ from the reference program's by a relative error of at most 0.018.
The reference program's roundings to bfloat16 on the way count: a program that leaves them out, or rounds other values in their place, can miss the bound.
Values may be sent and summed in bfloat16 or wider, within the bound.
No kernel may reach another device: no remote copies, remote signals or barrier semaphores. Data moves between devices by JAX's collectives and lax.ppermute only.
A program may use at most 448 MiB of HBM per device.

```python
import jax
import jax.numpy as jnp
from jax import lax

D = 2304
H = 8
KV = 4
HD = 256
FF = 9216
WINDOW = 4096
CAP = 50
SEQ_LEN = 8192
SEQS = 2
TOK_DEV = 2048


def draw_inputs(key, part):
    key = jax.random.fold_in(key, 3)
    base_key, row_key, column_key = jax.random.split(key, 3)
    shape = (SEQS, SEQ_LEN, D)
    base = jnp.clip(jax.random.normal(base_key, shape, jnp.float32), -4.0, 4.0)
    rows = jnp.exp(jax.random.uniform(row_key, (SEQS, SEQ_LEN, 1), jnp.float32, -1.15, 1.15))
    columns = jnp.exp(jax.random.uniform(column_key, (1, 1, D), jnp.float32, -1.15, 1.15))
    return (base * rows * columns).astype(jnp.bfloat16)


def draw_positions(key, part):
    key = jax.random.fold_in(key, 7)

    def one_row(row_key, row_number):
        keys = jax.random.split(row_key, 3)
        first = jax.random.randint(keys[0], (), 1, TOK_DEV // 2)
        second = first + jax.random.randint(keys[1], (), 1, TOK_DEV // 2)
        before = jnp.where(row_number == 0, 0, jax.random.randint(keys[2], (), 0, 3))
        ending = SEQ_LEN - TOK_DEV // 4
        index = jnp.arange(SEQ_LEN, dtype=jnp.int32)
        start = jnp.zeros((SEQ_LEN,), jnp.int32)
        start = jnp.where((before >= 1) & (index >= first), first, start)
        start = jnp.where((before >= 2) & (index >= second), second, start)
        start = jnp.where(index >= ending, ending, start)
        return (index - start).astype(jnp.int32)
    return jax.vmap(one_row)(jax.random.split(key, SEQS), jnp.arange(SEQS, dtype=jnp.int32))


def shard_levels(rng, dims, cuts, low, largest):
    level = 1.0
    for position, parts in cuts:
        draws = jax.random.uniform(jax.random.fold_in(jax.random.fold_in(rng, 6), position), (parts,), jnp.float32, low / len(cuts), largest / len(cuts))
        level = level * jnp.repeat(jnp.exp(draws), dims[position] // parts).reshape((-1,) + (1,) * (len(dims) - 1 - position))
    return level


def noise(key, dims, spread, most, cuts=(), held_as=jnp.bfloat16):
    level = shard_levels(key, dims, cuts, -0.22, 0.18) if cuts else 1.0
    array = jax.random.normal(key, dims, jnp.float32) * spread * level
    return jnp.minimum(jnp.maximum(array, -most), most).astype(held_as)


def setup_inputs(seed: int = 0) -> dict:
    streams_of = jax.random.split(jax.random.key(seed), 15)
    inputs = draw_inputs(jax.random.fold_in(streams_of[14], 71), 0)
    positions = draw_positions(jax.random.fold_in(streams_of[14], 71), 0)
    query_weight = noise(streams_of[2], (D, H * HD), (D // 3) ** -0.5, 0.21875, ((0, 8), (1, 4)))
    key_weight = noise(streams_of[3], (D, KV * HD), (D // 3) ** -0.5, 0.21875, ((0, 8), (1, 4)))
    value_weight = noise(streams_of[4], (D, KV * HD), D ** -0.5, 0.125, ((0, 8), (1, 4)))
    output_weight = noise(streams_of[5], (D, H * HD), (max(1, H * HD // 1024)) ** -0.5, 4.0, ((0, 8), (1, 4)))
    gate_weight = noise(streams_of[6], (D, FF), D ** -0.5, 0.125, ((0, 8), (1, 4)))
    up_weight = noise(streams_of[7], (D, FF), D ** -0.5, 0.125, ((0, 8), (1, 4)))
    down_weight = noise(streams_of[8], (D, FF), FF ** -0.5, 0.0625, ((0, 8), (1, 4)))
    pre_attention = jnp.clip(jax.random.uniform(streams_of[9], (D,), jnp.float32, -0.59765625, 0.59765625) * shard_levels(streams_of[9], (D,), ((0, 8),), -0.4, 0.0), -0.59765625, 0.59765625).astype(jnp.bfloat16)
    post_attention = jnp.clip(jax.random.uniform(streams_of[10], (D,), jnp.float32, -0.59765625, 0.59765625) * shard_levels(streams_of[10], (D,), ((0, 8),), -0.4, 0.0), -0.59765625, 0.59765625).astype(jnp.bfloat16)
    pre_feedforward = jnp.clip(jax.random.uniform(streams_of[11], (D,), jnp.float32, -0.59765625, 0.59765625) * shard_levels(streams_of[11], (D,), ((0, 8),), -0.4, 0.0), -0.59765625, 0.59765625).astype(jnp.bfloat16)
    post_feedforward = jnp.clip(jax.random.uniform(streams_of[12], (D,), jnp.float32, -0.59765625, 0.59765625) * shard_levels(streams_of[12], (D,), ((0, 8),), -0.4, 0.0), -0.59765625, 0.59765625).astype(jnp.bfloat16)
    cotangent = noise(streams_of[13], (SEQS, SEQ_LEN, D), 1.0, 6.0, ((0, 2), (1, 4)))
    return dict(inputs=inputs, positions=positions, query_weight=query_weight, key_weight=key_weight, value_weight=value_weight, output_weight=output_weight, gate_weight=gate_weight, up_weight=up_weight, down_weight=down_weight, pre_attention=pre_attention, post_attention=post_attention, pre_feedforward=pre_feedforward, post_feedforward=post_feedforward, cotangent=cotangent)


EPS = 1e-06
THETA = 10000.0
HIGH = lax.Precision.HIGHEST

@jax.custom_vjp
def low(v):
    return lax.optimization_barrier(v.astype(jnp.bfloat16)).astype(jnp.float32)

@jax.custom_vjp
def low_back(v):
    return v

def low_keep(v):
    return (low(v), None)

def low_pass(kept, grad):
    return (grad,)

def back_keep(v):
    return (v, None)

def back_low(kept, grad):
    return (low(grad),)
low.defvjp(low_keep, low_pass)
low_back.defvjp(back_keep, back_low)

def normalize(values, gain):
    factor = lax.rsqrt(lax.optimization_barrier(jnp.mean(values * values, axis=-1, keepdims=True)) + EPS)
    return values * factor * (1.0 + gain)

def gelu_tanh(values):
    return jax.nn.gelu(values, approximate=True)

def angles(places, width):
    half = width // 2
    frequency = jnp.power(THETA, -2.0 * jnp.arange(half, dtype=jnp.float32) / width)
    turned = places.astype(jnp.float32)[:, None] * frequency[None, :]
    return (jnp.cos(turned), jnp.sin(turned))

def rotate(values, cosine, sine):
    half = values.shape[-1] // 2
    first = values[..., :half]
    second = values[..., half:]
    cosine = cosine[:, None, :]
    sine = sine[:, None, :]
    return jnp.concatenate([first * cosine - second * sine, second * cosine + first * sine], axis=-1)

def attention(query_low, key_low, value_low, places):
    length = query_low.shape[0]
    block = min(512, length)
    blocks = length // block
    scale = HD ** (-0.5)
    padding = jnp.zeros((WINDOW, KV, HD), query_low.dtype)
    padded_keys = jnp.concatenate([padding, key_low], axis=0)
    padded_values = jnp.concatenate([padding, value_low], axis=0)
    query_blocks = query_low.reshape(blocks, block, KV, H // KV, HD)
    place_blocks = places.reshape(blocks, block)
    starts = jnp.arange(blocks, dtype=jnp.int32) * block
    spacing = WINDOW + jnp.arange(block, dtype=jnp.int32)[:, None] - jnp.arange(WINDOW + block, dtype=jnp.int32)[None, :]

    @jax.checkpoint
    def one_block(query_block, place_block, start):
        keys = lax.dynamic_slice_in_dim(padded_keys, start.astype(jnp.int32), WINDOW + block, 0)
        values = lax.dynamic_slice_in_dim(padded_values, start.astype(jnp.int32), WINDOW + block, 0)
        scores = low_back(jnp.einsum('qgrd,tgd->grqt', query_block, keys, precision=HIGH) * scale)
        bent = CAP * jnp.tanh(scores / CAP)
        allowed = (spacing >= 0) & (spacing <= place_block[:, None]) & (spacing < WINDOW)
        capped = jnp.where(allowed, bent, -1e+30)
        highest = lax.optimization_barrier(jnp.max(capped, axis=-1, keepdims=True))
        raised = jnp.exp(capped - highest)
        shares = low(raised / lax.optimization_barrier(jnp.sum(raised, axis=-1, keepdims=True)))
        return jnp.einsum('grqt,tgd->qgrd', shares, values, precision=HIGH).reshape(block, H * HD)
    heads = lax.map(lambda item: one_block(item[0], item[1], item[2]), (query_blocks, place_blocks, starts))
    return heads.reshape(length, H * HD)

def layer(hidden, places, weights):
    query_w, key_w, value_w, output_w, gate_w, up_w, down_w, gain_one, gain_two, gain_three, gain_four = weights
    length = hidden.shape[0]
    normed_one = low(normalize(hidden, gain_one))
    query_linear = low_back(jnp.dot(normed_one, query_w, precision=HIGH, preferred_element_type=jnp.float32))
    key_linear = low_back(jnp.dot(normed_one, key_w, precision=HIGH, preferred_element_type=jnp.float32))
    value_low = low_back(low(jnp.dot(normed_one, value_w, precision=HIGH, preferred_element_type=jnp.float32)))
    cosine, sine = angles(places, HD)
    query_low = low_back(low(rotate(query_linear.reshape(length, H, HD), cosine, sine)))
    key_low = low_back(low(rotate(key_linear.reshape(length, KV, HD), cosine, sine)))
    heads = attention(query_low, key_low, value_low.reshape(length, KV, HD), places)
    heads_low = low_back(low(heads))
    attention_out = low_back(jnp.dot(heads_low, output_w.T, precision=HIGH, preferred_element_type=jnp.float32))
    middle = hidden + normalize(attention_out, gain_two)
    normed_two = low(normalize(middle, gain_three))
    gate_linear = low_back(jnp.dot(normed_two, gate_w, precision=HIGH, preferred_element_type=jnp.float32))
    up_linear = low_back(jnp.dot(normed_two, up_w, precision=HIGH, preferred_element_type=jnp.float32))
    mixed = low(gelu_tanh(gate_linear) * up_linear)
    feedforward_out = low_back(jnp.dot(mixed, down_w.T, precision=HIGH, preferred_element_type=jnp.float32))
    return middle + normalize(feedforward_out, gain_four)

def reference(inputs, positions, query_weight, key_weight, value_weight, output_weight, gate_weight, up_weight, down_weight, pre_attention, post_attention, pre_feedforward, post_feedforward, cotangent):
    params = tuple((weight.astype(jnp.float32) for weight in (query_weight, key_weight, value_weight, output_weight, gate_weight, up_weight, down_weight, pre_attention, post_attention, pre_feedforward, post_feedforward)))

    def whole(hidden, weights):

        @jax.checkpoint
        def one_sequence(item):
            return layer(item[0], item[1], weights)
        return lax.map(one_sequence, (hidden, positions))
    result, backward = jax.vjp(whole, inputs.astype(jnp.float32), params)
    input_gradient, grads = backward(cotangent.astype(jnp.float32))
    return (result.astype(jnp.bfloat16), input_gradient, grads[0], grads[1], grads[2], grads[3], grads[4], grads[5], grads[6], grads[7], grads[8], grads[9], grads[10])
```

```python
import functools

import jax
import jax.numpy as jnp
from jax import lax
from jax.experimental import pallas as pl
from jax.experimental.pallas import tpu as pltpu
from jax.sharding import PartitionSpec as P

HD = 256
WINDOW = 4096
CAP = 50
EPS = 1e-06
KEYS = 512
LOG2E = 1.4426950408889634
BEND = HD ** (-0.5) / CAP
RAISE = CAP * LOG2E
GELU = 0.7978845608028654
NT = (((1,), (1,)), ((), ()))
TN = (((0,), (0,)), ((), ()))
SMALL = pl.CostEstimate(flops=1, bytes_accessed=1, transcendentals=0)


def rotate(values, cosine, sine):
    half = HD // 2
    first, second = values[:, :half], values[:, half:]
    return jnp.concatenate([first * cosine - second * sine, second * cosine + first * sine], axis=1)


def stack_heads(block):
    return jnp.concatenate([block[:, :HD], block[:, HD:]], axis=0)


def load_pieces(pieces, window_ref, sems):
    rows = pieces[0].shape[0]
    copies = [
        pltpu.make_async_copy(piece, window_ref.at[pl.ds(i * rows, rows)], sems.at[i]) for i, piece in enumerate(pieces)
    ]
    for copy in copies:
        copy.start()
    for copy in copies:
        copy.wait()


def attend_kernel(first, number, bounds_ref, query_ref, low_ref, *rest):
    pieces, (heads_ref, stat_ref, acc_ref, sum_ref, window_ref, sems) = rest[:number], rest[number:]
    step = pl.program_id(0)

    @pl.when(step == 0)
    def _():
        load_pieces(pieces, window_ref, sems)

    chunk = query_ref.shape[0]
    base = (first + step) * chunk
    query = stack_heads(query_ref[...])
    acc_ref[...] = jnp.zeros_like(acc_ref)
    sum_ref[...] = jnp.zeros_like(sum_ref)

    def add_block(offset, size, masked, causal):
        rows = pl.ds(pl.multiple_of(base + offset, 256), size)
        keys = window_ref[rows, :HD]
        values = window_ref[rows, HD:]
        scores = lax.dot_general(query, keys, NT, preferred_element_type=jnp.float32)
        raised = jnp.exp2(jnp.tanh(scores * BEND) * RAISE)
        if masked:
            column = offset + lax.broadcasted_iota(jnp.int32, (chunk, size), 1)
            keep = column >= jnp.concatenate([low_ref[...]] * (size // 128), axis=1)
            if causal:
                keep &= column <= WINDOW + lax.broadcasted_iota(jnp.int32, (chunk, size), 0)
            raised = jnp.where(jnp.concatenate([keep, keep], axis=0), raised, 0.0)
        part = raised[:, :128]
        for lane in range(128, size, 128):
            part = part + raised[:, lane : lane + 128]
        sum_ref[...] += part
        acc_ref[...] += jnp.dot(raised.astype(jnp.bfloat16), values, preferred_element_type=jnp.float32)

    def masked_step(block, carry):
        add_block(block * KEYS, KEYS, True, False)
        return carry

    def full_step(block, carry):
        add_block(block * KEYS, KEYS, False, False)
        return carry

    blocks = WINDOW // KEYS
    lax.fori_loop(bounds_ref[first + step, 0], bounds_ref[first + step, 1], masked_step, 0)
    lax.fori_loop(bounds_ref[first + step, 1], blocks, full_step, 0)
    add_block(WINDOW, chunk, True, True)
    total = jnp.sum(sum_ref[...], axis=1, keepdims=True)
    heads = (acc_ref[...] / total).astype(jnp.bfloat16)
    heads_ref[:, :HD] = heads[:chunk]
    heads_ref[:, HD:] = heads[chunk:]
    stat_ref[...] = jnp.broadcast_to(jnp.log2(total), stat_ref.shape)


def attend(query, pieces, low, bounds, first, count, chunk):
    rows = count * chunk
    span = len(pieces) * pieces[0].shape[0]
    return pl.pallas_call(
        functools.partial(attend_kernel, first, len(pieces)),
        out_shape=(
            jax.ShapeDtypeStruct((rows, 2 * HD), jnp.bfloat16),
            jax.ShapeDtypeStruct((2 * rows, 128), jnp.float32),
        ),
        grid_spec=pltpu.PrefetchScalarGridSpec(
            num_scalar_prefetch=1,
            grid=(count,),
            in_specs=[
                pl.BlockSpec((chunk, 2 * HD), lambda g, b: (first + g, 0)),
                pl.BlockSpec((chunk, 128), lambda g, b: (first + g, 0)),
            ]
            + [pl.BlockSpec(memory_space=pl.ANY)] * len(pieces),
            out_specs=[
                pl.BlockSpec((chunk, 2 * HD), lambda g, b: (g, 0)),
                pl.BlockSpec((2 * chunk, 128), lambda g, b: (g, 0)),
            ],
            scratch_shapes=[
                pltpu.VMEM((2 * chunk, HD), jnp.float32),
                pltpu.VMEM((2 * chunk, 128), jnp.float32),
                pltpu.VMEM((span, 2 * HD), jnp.bfloat16),
                pltpu.SemaphoreType.DMA((len(pieces),)),
            ],
        ),
        compiler_params=pltpu.CompilerParams(vmem_limit_bytes=48 * 2**20),
        cost_estimate=SMALL,
        name="attend",
    )(bounds, query, low, *pieces)


def attend_back_kernel(
    first, number, carried, sent, bounds_ref, query_ref, grad_ref, heads_ref, stat_ref, low_ref, cosine_ref, sine_ref, *rest
):
    pieces, rest = rest[:number], rest[number:]
    if carried:
        before_ref, *rest = rest
    dquery_ref, *afters, sum_ref, acc_ref, window_ref, sem, sems = rest
    step = pl.program_id(0)
    chunk = query_ref.shape[0]
    base = (first + step) * chunk

    @pl.when(step == 0)
    def _():
        if carried:
            copy = pltpu.make_async_copy(before_ref, sum_ref, sem)
            copy.start()
        else:
            sum_ref[...] = jnp.zeros_like(sum_ref)
        load_pieces(pieces, window_ref, sems)
        if carried:
            copy.wait()

    query = stack_heads(query_ref[...])
    grad = stack_heads(grad_ref[...])
    heads = stack_heads(heads_ref[...])
    inner = jnp.sum(grad.astype(jnp.float32) * heads.astype(jnp.float32), axis=1, keepdims=True)
    inner = jnp.broadcast_to(inner, (2 * chunk, 128)).T[:1]
    stat = stat_ref[...].T[:1]
    low = low_ref[...]
    low = jnp.concatenate([low, low], axis=1)
    acc_ref[...] = jnp.zeros_like(acc_ref)

    def add_block(offset, size, masked, causal):
        place = pl.multiple_of(base + offset, 256)
        rows = pl.ds(place, size)
        keys = window_ref[rows, :HD]
        values = window_ref[rows, HD:]
        scores = lax.dot_general(keys, query, NT, preferred_element_type=jnp.float32)
        slope = jnp.tanh(scores * BEND)
        shares = jnp.exp2(slope * RAISE - stat)
        if masked:
            row = offset + lax.broadcasted_iota(jnp.int32, (size, 2 * chunk), 0)
            keep = row >= low
            if causal:
                column = lax.broadcasted_iota(jnp.int32, (size, chunk), 1)
                keep &= row <= WINDOW + jnp.concatenate([column, column], axis=1)
            shares = jnp.where(keep, shares, 0.0)
        share_grad = lax.dot_general(values, grad, NT, preferred_element_type=jnp.float32)
        score_low = (shares * (share_grad - inner) * (1.0 - slope * slope)).astype(jnp.bfloat16)
        sum_ref[rows, HD:] += jnp.dot(shares.astype(jnp.bfloat16), grad, preferred_element_type=jnp.float32)
        sum_ref[rows, :HD] += jnp.dot(score_low, query, preferred_element_type=jnp.float32)
        acc_ref[...] += lax.dot_general(keys, score_low, TN, preferred_element_type=jnp.float32)

    def masked_step(block, carry):
        add_block(block * KEYS, KEYS, True, False)
        return carry

    def full_step(block, carry):
        add_block(block * KEYS, KEYS, False, False)
        return carry

    blocks = WINDOW // KEYS
    lax.fori_loop(bounds_ref[first + step, 0], bounds_ref[first + step, 1], masked_step, 0)
    lax.fori_loop(bounds_ref[first + step, 1], blocks, full_step, 0)
    add_block(WINDOW, chunk, True, True)
    dquery = (acc_ref[...].T * HD ** (-0.5)).astype(jnp.bfloat16).astype(jnp.float32)
    for head in range(2):
        turned = rotate(dquery[head * chunk : (head + 1) * chunk], cosine_ref[...], -sine_ref[...])
        dquery_ref[:, head * HD : (head + 1) * HD] = turned.astype(jnp.bfloat16)

    @pl.when(step == pl.num_programs(0) - 1)
    def _():
        done = 0
        for out in afters[:-1]:
            out[...] = sum_ref[done : done + out.shape[0], :].astype(jnp.bfloat16)
            done += out.shape[0]
        copy = pltpu.make_async_copy(sum_ref.at[pl.ds(done, sum_ref.shape[0] - done)], afters[-1], sem)
        copy.start()
        copy.wait()


def attend_back(query, grad, heads, stat, pieces, low_row, cosine, sine, bounds, before, first, count, chunk,
                sent):
    rows = count * chunk
    span = len(pieces) * pieces[0].shape[0]
    carried = before is not None
    extra = [before] if carried else []
    return pl.pallas_call(
        functools.partial(attend_back_kernel, first, len(pieces), carried, sent),
        out_shape=(
            jax.ShapeDtypeStruct((rows, 2 * HD), jnp.bfloat16),
            *(jax.ShapeDtypeStruct((size, 2 * HD), jnp.bfloat16) for size in sent),
            jax.ShapeDtypeStruct((span - sum(sent), 2 * HD), jnp.float32),
        ),
        grid_spec=pltpu.PrefetchScalarGridSpec(
            num_scalar_prefetch=1,
            grid=(count,),
            in_specs=[
                pl.BlockSpec((chunk, 2 * HD), lambda g, b: (first + g, 0)),
                pl.BlockSpec((chunk, 2 * HD), lambda g, b: (g, 0)),
                pl.BlockSpec((chunk, 2 * HD), lambda g, b: (g, 0)),
                pl.BlockSpec((2 * chunk, 128), lambda g, b: (g, 0)),
                pl.BlockSpec((1, chunk), lambda g, b: (0, first + g)),
                pl.BlockSpec((chunk, HD // 2), lambda g, b: (first + g, 0)),
                pl.BlockSpec((chunk, HD // 2), lambda g, b: (first + g, 0)),
            ]
            + [pl.BlockSpec(memory_space=pl.ANY)] * (len(pieces) + len(extra)),
            out_specs=[
                pl.BlockSpec((chunk, 2 * HD), lambda g, b: (g, 0)),
                *(pl.BlockSpec((size, 2 * HD), lambda g, b: (0, 0)) for size in sent),
                pl.BlockSpec(memory_space=pl.ANY),
            ],
            scratch_shapes=[
                pltpu.VMEM((span, 2 * HD), jnp.float32),
                pltpu.VMEM((HD, 2 * chunk), jnp.float32),
                pltpu.VMEM((span, 2 * HD), jnp.bfloat16),
                pltpu.SemaphoreType.DMA,
                pltpu.SemaphoreType.DMA((len(pieces),)),
            ],
        ),
        compiler_params=pltpu.CompilerParams(vmem_limit_bytes=60 * 2**20),
        cost_estimate=SMALL,
        name="attend_back",
    )(bounds, query, grad, heads, stat, low_row, cosine, sine, *pieces, *extra)


def limits(places, chunk):
    count = places.shape[0] // chunk
    low = WINDOW + jnp.arange(chunk, dtype=jnp.int32)[None, :] - jnp.minimum(places.reshape(count, chunk), WINDOW - 1)
    blocks = WINDOW // KEYS
    begin = jnp.minimum(jnp.min(low, axis=1) // KEYS, blocks)
    full = jnp.minimum((jnp.max(low, axis=1) + KEYS - 1) // KEYS, blocks)
    return low.reshape(-1), jnp.stack([begin, full], axis=1)


def scaled(values):
    factor = lax.rsqrt(jnp.mean(values * values, axis=-1, keepdims=True) + EPS)
    return factor, values * factor


def project_group_kernel(hidden_ref, gain_ref, weight_ref, cosine_ref, sine_ref, normed_ref, own_ref, factor_ref):
    factor, normed = scaled(hidden_ref[...].astype(jnp.float32))
    factor_ref[...] = jnp.broadcast_to(factor, factor_ref.shape)
    normed = (normed * gain_ref[...]).astype(jnp.bfloat16)
    normed_ref[...] = normed
    linear = jnp.dot(normed, weight_ref[...], preferred_element_type=jnp.float32)
    own_ref[:, :HD] = rotate(linear[:, :HD], cosine_ref[...], sine_ref[...]).astype(jnp.bfloat16)
    own_ref[:, HD:] = linear[:, HD:].astype(jnp.bfloat16)


def project_group(hidden, gain, weight, cosine, sine):
    rows, features = hidden.shape
    tile = min(256, rows)
    return pl.pallas_call(
        project_group_kernel,
        out_shape=(
            jax.ShapeDtypeStruct((rows, features), jnp.bfloat16),
            jax.ShapeDtypeStruct((rows, 2 * HD), jnp.bfloat16),
            jax.ShapeDtypeStruct((rows, 128), jnp.float32),
        ),
        grid=(rows // tile,),
        in_specs=[
            pl.BlockSpec((tile, features), lambda g: (g, 0)),
            pl.BlockSpec((1, features), lambda g: (0, 0)),
            pl.BlockSpec((features, 2 * HD), lambda g: (0, 0), pipeline_mode=pl.Buffered(1)),
            pl.BlockSpec((tile, HD // 2), lambda g: (g, 0)),
            pl.BlockSpec((tile, HD // 2), lambda g: (g, 0)),
        ],
        out_specs=[
            pl.BlockSpec((tile, features), lambda g: (g, 0)),
            pl.BlockSpec((tile, 2 * HD), lambda g: (g, 0)),
            pl.BlockSpec((tile, 128), lambda g: (g, 0)),
        ],
        compiler_params=pltpu.CompilerParams(vmem_limit_bytes=32 * 2**20),
        cost_estimate=SMALL,
        name="project_group",
    )(hidden, gain, weight, cosine, sine)


def project_heads_kernel(normed_ref, weight_ref, cosine_ref, sine_ref, query_ref):
    linear = jnp.dot(normed_ref[...], weight_ref[...], preferred_element_type=jnp.float32)
    for head in range(0, 2 * HD, HD):
        turned = rotate(linear[:, head : head + HD], cosine_ref[...], sine_ref[...])
        query_ref[:, head : head + HD] = turned.astype(jnp.bfloat16)


def project_heads(normed, weight, cosine, sine):
    rows, features = normed.shape
    tile = min(256, rows)
    return pl.pallas_call(
        project_heads_kernel,
        out_shape=jax.ShapeDtypeStruct((rows, 2 * HD), jnp.bfloat16),
        grid=(rows // tile,),
        in_specs=[
            pl.BlockSpec((tile, features), lambda g: (g, 0)),
            pl.BlockSpec((features, 2 * HD), lambda g: (0, 0), pipeline_mode=pl.Buffered(1)),
            pl.BlockSpec((tile, HD // 2), lambda g: (g, 0)),
            pl.BlockSpec((tile, HD // 2), lambda g: (g, 0)),
        ],
        out_specs=pl.BlockSpec((tile, 2 * HD), lambda g: (g, 0)),
        compiler_params=pltpu.CompilerParams(vmem_limit_bytes=32 * 2**20),
        cost_estimate=SMALL,
        name="project_heads",
    )(normed, weight, cosine, sine)


def finish_group_kernel(cosine_ref, sine_ref, own_ref, *rest):
    *arrived, low_ref = rest
    total = own_ref[...]
    for block in arrived:
        total = total + block[...].astype(jnp.float32)
    key_rot = (total[:, :HD] * HD ** (-0.5)).astype(jnp.bfloat16).astype(jnp.float32)
    low_ref[:, :HD] = rotate(key_rot, cosine_ref[...], -sine_ref[...]).astype(jnp.bfloat16)
    low_ref[:, HD:] = total[:, HD:].astype(jnp.bfloat16)


def finish_group(sums, arrived, cosine, sine, index):
    rows = arrived[0].shape[0]
    tile = min(256, rows)
    skip = index * (rows // tile)
    wide = pl.BlockSpec((tile, 2 * HD), lambda g: (g, 0))
    half = pl.BlockSpec((tile, HD // 2), lambda g: (skip + g, 0))
    return pl.pallas_call(
        finish_group_kernel,
        out_shape=jax.ShapeDtypeStruct((rows, 2 * HD), jnp.bfloat16),
        grid=(rows // tile,),
        in_specs=[half, half, pl.BlockSpec((tile, 2 * HD), lambda g: (skip + g, 0))] + [wide] * len(arrived),
        out_specs=wide,
        cost_estimate=SMALL,
        name="finish_group",
    )(cosine, sine, sums, *arrived)


ROW = 64
TILE = 256
WIDE = 768
GATE_TILE = 384


def pick(middle, total_ref, outward_ref, rows):
    total = jnp.where(middle, total_ref[rows, :].astype(jnp.float32), outward_ref[rows, :].astype(jnp.float32))
    return total


def fold(values):
    return jnp.sum(values.reshape(-1, 8, values.shape[1]), axis=0)


def gate_kernel(number, chunk, middle_ref, *rest):
    came, rest = rest[: 2 * number], rest[2 * number :]
    hidden_ref, gains_ref, gate_weight_ref, up_weight_ref, *rest = rest
    attended_ref, between_ref, normed_ref, gate_ref, up_ref, mixed_ref = rest
    middle = middle_ref[0] == 1

    @pl.when(pl.program_id(0) == 0)
    def _():
        for i in range(number):

            def step(r, carry):
                rows = pl.ds(pl.multiple_of(r * ROW, ROW), ROW)
                place = pl.ds(pl.multiple_of(i * chunk + r * ROW, ROW), ROW)
                attended = pick(middle, came[2 * i], came[2 * i + 1], rows)
                between = hidden_ref[place, :].astype(jnp.float32) + scaled(attended)[1] * gains_ref[1:2, :]
                attended_ref[place, :] = attended.astype(jnp.bfloat16)
                between_ref[place, :] = between
                normed_ref[place, :] = (scaled(between)[1] * gains_ref[2:3, :]).astype(jnp.bfloat16)
                return carry

            lax.fori_loop(0, chunk // ROW, step, 0)

    gate = jnp.dot(normed_ref[...], gate_weight_ref[...], preferred_element_type=jnp.float32)
    up = jnp.dot(normed_ref[...], up_weight_ref[...], preferred_element_type=jnp.float32)
    gate_ref[...] = gate
    up_ref[...] = up
    mixed_ref[...] = (jax.nn.gelu(gate, approximate=True) * up).astype(jnp.bfloat16)


def full_block(rows, columns):
    return pl.BlockSpec((rows, columns), lambda n, m: (0, 0))


def gate_call(middle, came, hidden, gains, gate_weight, up_weight, pair):
    number = len(came) // 2
    chunk, features = came[0].shape
    rows = number * chunk
    units = gate_weight.shape[1]
    wide = pl.BlockSpec((features, GATE_TILE), lambda n, m: (0, n))
    tall = pl.BlockSpec((rows, GATE_TILE), lambda n, m: (0, n))
    return pl.pallas_call(
        functools.partial(gate_kernel, number, chunk),
        out_shape=(
            jax.ShapeDtypeStruct((rows, features), jnp.bfloat16),
            jax.ShapeDtypeStruct((rows, features), jnp.float32),
            jax.ShapeDtypeStruct((rows, features), jnp.bfloat16),
            jax.ShapeDtypeStruct((rows, units), jnp.float32),
            jax.ShapeDtypeStruct((rows, units), jnp.float32),
            jax.ShapeDtypeStruct((rows, units), jnp.bfloat16),
        ),
        grid_spec=pltpu.PrefetchScalarGridSpec(
            num_scalar_prefetch=1,
            grid=(units // GATE_TILE,),
            in_specs=[full_block(chunk, features)] * len(came)
            + [pl.BlockSpec((rows, features), lambda n, m: (pair, 0)), full_block(4, features), wide, wide],
            out_specs=[full_block(rows, features)] * 3 + [tall] * 3,
        ),
        compiler_params=pltpu.CompilerParams(vmem_limit_bytes=60 * 2**20),
        cost_estimate=SMALL,
        name="gate",
    )(middle, *came, hidden, gains, gate_weight, up_weight)


def back_out_kernel(number, chunk, *rest):
    terms, outs = rest[:-number], rest[-number:]
    total = 0.0
    for left, weight in zip(terms[::2], terms[1::2]):
        total = total + lax.dot_general(left[...], weight[...], NT, preferred_element_type=jnp.float32)
    total = total.astype(jnp.bfloat16)
    for i, out in enumerate(outs):
        out[...] = total[i * chunk : (i + 1) * chunk]


def back_out(terms, chunk):
    rows, units = terms[0][0].shape
    features = terms[0][1].shape[0]
    number = rows // chunk
    left = pl.BlockSpec((rows, units), lambda n: (0, 0))
    weight = pl.BlockSpec((WIDE, units), lambda n: (n, 0))
    return pl.pallas_call(
        functools.partial(back_out_kernel, number, chunk),
        out_shape=[jax.ShapeDtypeStruct((chunk, features), jnp.bfloat16)] * number,
        grid=(features // WIDE,),
        in_specs=[left, weight] * len(terms),
        out_specs=[pl.BlockSpec((chunk, WIDE), lambda n: (0, n))] * number,
        compiler_params=pltpu.CompilerParams(vmem_limit_bytes=48 * 2**20),
        cost_estimate=SMALL,
        name="back_out",
    )(*[array for term in terms for array in term])


def mixed_back_kernel(number, chunk, middle_ref, *rest):
    came, rest = rest[: 2 * number], rest[2 * number :]
    between_ref, upstream_ref, gains_ref, down_ref, gate_ref, up_ref, *rest = rest
    result_ref, fed_ref, gain_ref, gate_low_ref, up_low_ref = rest[-5:]
    middle = middle_ref[0] == 1

    @pl.when(pl.program_id(0) == 0)
    def _():
        gain_ref[...] = jnp.zeros_like(gain_ref)
        for i in range(number):

            def step(r, carry):
                rows = pl.ds(pl.multiple_of(r * ROW, ROW), ROW)
                place = pl.ds(pl.multiple_of(i * chunk + r * ROW, ROW), ROW)
                factor, normed = scaled(pick(middle, came[2 * i], came[2 * i + 1], rows))
                raised = normed * gains_ref[3:4, :]
                result_ref[place, :] = (between_ref[place, :] + raised).astype(jnp.bfloat16)
                given = upstream_ref[place, :].astype(jnp.float32)
                gain_ref[...] += fold(given * normed)
                inner = jnp.mean(given * raised, axis=-1, keepdims=True)
                fed_ref[place, :] = (factor * (given * gains_ref[3:4, :] - normed * inner)).astype(jnp.bfloat16)
                return carry

            lax.fori_loop(0, chunk // ROW, step, 0)

    mixed_grad = jnp.dot(fed_ref[...], down_ref[...], preferred_element_type=jnp.float32)
    gate = gate_ref[...]
    inside = GELU * (gate + 0.044715 * gate * gate * gate)
    bent = jnp.tanh(inside)
    half = 0.5 * (1.0 + bent)
    slope = half + 0.5 * gate * (1.0 - bent * bent) * (GELU * (1.0 + 3 * 0.044715 * gate * gate))
    gate_low_ref[...] = (mixed_grad * up_ref[...] * slope).astype(jnp.bfloat16)
    up_low_ref[...] = (mixed_grad * (gate * half)).astype(jnp.bfloat16)


def mixed_back(middle, came, between, upstream, gains, down_weight, gate, up, pair, before):
    number = len(came) // 2
    chunk, features = came[0].shape
    rows = number * chunk
    units = down_weight.shape[1]
    tall = pl.BlockSpec((rows, GATE_TILE), lambda n, m: (0, n))
    extra = [] if before is None else [before]
    return pl.pallas_call(
        functools.partial(mixed_back_kernel, number, chunk),
        out_shape=(
            jax.ShapeDtypeStruct(upstream.shape, jnp.bfloat16),
            jax.ShapeDtypeStruct((rows, features), jnp.bfloat16),
            jax.ShapeDtypeStruct((8, features), jnp.float32),
            jax.ShapeDtypeStruct((rows, units), jnp.bfloat16),
            jax.ShapeDtypeStruct((rows, units), jnp.bfloat16),
        ),
        grid_spec=pltpu.PrefetchScalarGridSpec(
            num_scalar_prefetch=1,
            grid=(units // GATE_TILE,),
            in_specs=[full_block(chunk, features)] * len(came)
            + [
                full_block(rows, features),
                pl.BlockSpec((rows, features), lambda n, m: (pair, 0)),
                full_block(4, features),
                pl.BlockSpec((features, GATE_TILE), lambda n, m: (0, n)),
                tall,
                tall,
            ]
            + [pl.BlockSpec(memory_space=pl.ANY)] * len(extra),
            out_specs=[pl.BlockSpec((rows, features), lambda n, m: (pair, 0)), full_block(rows, features)]
            + [full_block(8, features)]
            + [tall] * 2,
        ),
        input_output_aliases={} if before is None else {len(came) + 7: 0},
        compiler_params=pltpu.CompilerParams(vmem_limit_bytes=60 * 2**20),
        cost_estimate=SMALL,
        name="mixed_back",
    )(middle, *came, between, upstream, gains, down_weight, gate, up, *extra)


def attention_low_kernel(middle_ref, *rest):
    came, rest = rest[:4], rest[4:]
    (between_ref, attended_ref, upstream_ref, gains_ref, weight_ref,
     grad_ref, low_ref, gain_two_ref, gain_three_ref, heads_ref) = rest
    middle = middle_ref[0] == 1
    step = pl.program_id(0)
    early = step < pl.num_programs(0) // 2
    size = between_ref.shape[0]

    @pl.when(step == 0)
    def _():
        gain_two_ref[...] = jnp.zeros_like(gain_two_ref)
        gain_three_ref[...] = jnp.zeros_like(gain_three_ref)

    rows = pl.ds(0, size)
    total = jnp.where(early, pick(middle, came[0], came[1], rows), pick(middle, came[2], came[3], rows))
    factor, normed = scaled(between_ref[...])
    gain_three_ref[...] += fold(total * normed)
    raised = total * gains_ref[2:3, :]
    inner = jnp.mean(raised * normed, axis=-1, keepdims=True)
    grad = upstream_ref[...].astype(jnp.float32) + factor * (raised - normed * inner)
    grad_ref[...] = grad
    factor, normed = scaled(attended_ref[...].astype(jnp.float32))
    gain_two_ref[...] += fold(grad * normed)
    raised = grad * gains_ref[1:2, :]
    inner = jnp.mean(raised * normed, axis=-1, keepdims=True)
    low_ref[pl.ds(pl.multiple_of(step * size, size), size), :] = (factor * (raised - normed * inner)).astype(jnp.bfloat16)

    @pl.when(step == pl.num_programs(0) - 1)
    def _():
        heads = jnp.dot(low_ref[...], weight_ref[...], preferred_element_type=jnp.float32)
        heads_ref[...] = heads.astype(jnp.bfloat16)


def attention_low(middle, came, between, attended, upstream, gains, weight, index):
    chunk, features = between.shape
    width = weight.shape[1]
    size = ROW
    parts = chunk // size

    def some(offset):
        return pl.BlockSpec((size, features), lambda n, m: (offset * parts + n, 0))

    first = pl.BlockSpec((size, features), lambda n, m: (jnp.minimum(n, parts // 2 - 1), 0))
    second = pl.BlockSpec((size, features), lambda n, m: (jnp.maximum(n - parts // 2, 0), 0))
    return pl.pallas_call(
        attention_low_kernel,
        out_shape=(
            jax.ShapeDtypeStruct((chunk, features), jnp.float32),
            jax.ShapeDtypeStruct((chunk, features), jnp.bfloat16),
            jax.ShapeDtypeStruct((8, features), jnp.float32),
            jax.ShapeDtypeStruct((8, features), jnp.float32),
            jax.ShapeDtypeStruct((chunk, width), jnp.bfloat16),
        ),
        grid_spec=pltpu.PrefetchScalarGridSpec(
            num_scalar_prefetch=1,
            grid=(parts,),
            in_specs=[
                first, first, second, second, some(0), some(0), some(index), full_block(4, features),
                full_block(features, width),
            ],
            out_specs=[
                some(0), full_block(chunk, features), full_block(8, features), full_block(8, features),
                full_block(chunk, width),
            ],
        ),
        compiler_params=pltpu.CompilerParams(vmem_limit_bytes=48 * 2**20),
        cost_estimate=SMALL,
        name="attention_low",
    )(middle, *came, between, attended, upstream, gains, weight)


def share_kernel(number, *rest):
    lefts, rights, (out_ref, turned_ref, right_ref, sems) = rest[:number], rest[number : 2 * number], rest[2 * number :]
    rows = lefts[0].shape[0]

    @pl.when(pl.program_id(0) == 0)
    def _():
        load_pieces(rights, right_ref, sems)

    for i, left in enumerate(lefts):
        turned_ref[:, i * rows : (i + 1) * rows] = left[...].T
    out = jnp.dot(turned_ref[...], right_ref[...], preferred_element_type=jnp.float32)
    out_ref[...] = out.astype(jnp.bfloat16)


def share_call(lefts, rights):
    number = len(rights)
    rows, columns = rights[0].shape
    features = lefts[0].shape[1]
    cut = len(lefts) == 1 and number > 1
    lefts = lefts * number if cut else lefts
    return pl.pallas_call(
        functools.partial(share_kernel, number),
        out_shape=jax.ShapeDtypeStruct((features, columns), jnp.bfloat16),
        grid=(features // TILE,),
        in_specs=[pl.BlockSpec((rows, TILE), lambda n, i=i * cut: (i, n)) for i in range(number)]
        + [pl.BlockSpec(memory_space=pl.ANY)] * number,
        out_specs=pl.BlockSpec((TILE, columns), lambda n: (n, 0)),
        scratch_shapes=[
            pltpu.VMEM((TILE, number * rows), jnp.bfloat16),
            pltpu.VMEM((number * rows, columns), jnp.bfloat16),
            pltpu.SemaphoreType.DMA((number,)),
        ],
        compiler_params=pltpu.CompilerParams(vmem_limit_bytes=48 * 2**20),
        cost_estimate=SMALL,
        name="share",
    )(*lefts, *rights)


def pair_sums_kernel(*refs):
    number = len(refs) // 3
    for i in range(number):
        left, right, out = refs[2 * i], refs[2 * i + 1], refs[2 * number + i]
        out[...] = (left[...].astype(jnp.float32) + right[...].astype(jnp.float32)).astype(jnp.bfloat16)


def pair_sums(pairs):
    rows, columns = pairs[0][0].shape
    tile = min(rows, ROW)
    block = pl.BlockSpec((tile, columns), lambda g: (g, 0))
    return pl.pallas_call(
        pair_sums_kernel,
        out_shape=[jax.ShapeDtypeStruct((rows, columns), jnp.bfloat16)] * len(pairs),
        grid=(rows // tile,),
        in_specs=[block] * (2 * len(pairs)),
        out_specs=[block] * len(pairs),
        cost_estimate=SMALL,
        name="pair_sums",
    )(*[array for pair in pairs for array in pair])


def linear_back_kernel(query_grad_ref, group_ref, query_ref, weight_ref, hidden_ref, factor_ref, one_ref, two_ref, gain_ref):
    partial = lax.dot_general(query_grad_ref[...], query_ref[...], NT, preferred_element_type=jnp.float32)
    partial += lax.dot_general(group_ref[...], weight_ref[...], NT, preferred_element_type=jnp.float32)
    normed = hidden_ref[...].astype(jnp.float32) * factor_ref[:, :1]
    gain_ref[...] = fold(partial * normed)
    half = one_ref.shape[0]
    partial = partial.astype(jnp.bfloat16)
    one_ref[...] = partial[:half]
    two_ref[...] = partial[half:]


def linear_back(query_grad, query_block, group, group_block, query_weight, group_weight, hidden, factor, index, rows):
    features, width = query_weight.shape
    tile = WIDE
    row = pl.BlockSpec((rows, tile), lambda n: (index, n))
    weight = pl.BlockSpec((tile, width), lambda n: (n, 0))
    half = pl.BlockSpec((rows // 2, tile), lambda n: (0, n))
    return pl.pallas_call(
        linear_back_kernel,
        out_shape=(
            jax.ShapeDtypeStruct((rows // 2, features), jnp.bfloat16),
            jax.ShapeDtypeStruct((rows // 2, features), jnp.bfloat16),
            jax.ShapeDtypeStruct((8, features), jnp.float32),
        ),
        grid=(features // tile,),
        in_specs=[
            pl.BlockSpec((rows, width), lambda n: (query_block, 0)),
            pl.BlockSpec((rows, width), lambda n: (group_block, 0)),
            weight,
            weight,
            row,
            pl.BlockSpec((rows, 128), lambda n: (index, 0)),
        ],
        out_specs=[half, half, pl.BlockSpec((8, tile), lambda n: (0, n))],
        compiler_params=pltpu.CompilerParams(vmem_limit_bytes=32 * 2**20),
        cost_estimate=SMALL,
        name="linear_back",
    )(query_grad, group, query_weight, group_weight, hidden, factor)


def input_grad_kernel(middle_ref, *rest):
    came, (hidden_ref, upper_ref, gains_ref, *ignored, out_ref) = rest[:4], rest[4:]
    middle = middle_ref[0] == 1
    early = pl.program_id(0) < pl.num_programs(0) // 2
    rows = pl.ds(0, hidden_ref.shape[0])
    total = jnp.where(early, pick(middle, came[0], came[1], rows), pick(middle, came[2], came[3], rows))
    factor, normed = scaled(hidden_ref[...].astype(jnp.float32))
    raised = total * gains_ref[0:1, :]
    inner = jnp.mean(raised * normed, axis=-1, keepdims=True)
    out_ref[...] = upper_ref[...] + factor * (raised - normed * inner)


def input_grad(middle, came, hidden, upper, upper_block, gains, index, before):
    half, features = came[0].shape
    size = min(ROW, half)
    parts = 2 * half // size

    def some(block):
        return pl.BlockSpec((size, features), lambda n, m: (block * parts + n, 0))

    first = pl.BlockSpec((size, features), lambda n, m: (jnp.minimum(n, parts // 2 - 1), 0))
    second = pl.BlockSpec((size, features), lambda n, m: (jnp.maximum(n - parts // 2, 0), 0))
    extra = [] if before is None else [before]
    return pl.pallas_call(
        input_grad_kernel,
        out_shape=jax.ShapeDtypeStruct(hidden.shape, jnp.float32),
        grid_spec=pltpu.PrefetchScalarGridSpec(
            num_scalar_prefetch=1,
            grid=(parts,),
            in_specs=[first, first, second, second, some(index), some(upper_block), full_block(4, features)]
            + [pl.BlockSpec(memory_space=pl.ANY)] * len(extra),
            out_specs=some(index),
        ),
        input_output_aliases={8: 0} if extra else {},
        compiler_params=pltpu.CompilerParams(vmem_limit_bytes=32 * 2**20),
        cost_estimate=SMALL,
        name="input_grad",
    )(middle, *came, hidden, upper, gains, *extra)


THETA = 10000.0
ROWS = ("dp", "seq")
LINE = "tensor"
LOW = jnp.bfloat16
FULL = jnp.float32
CHUNK = 512
FINE = 256
BUDGET = 48.0
FINE_BUDGET = 30.0
(HEADS, STAT, ATTENDED, BETWEEN, NORMED, GATE, UP, MIXED, FED, RESULT, FED_LOW, GAIN_ONE, GAIN_TWO, GAIN_THREE,
 GAIN_FOUR, GATE_LOW, UP_LOW, NORMED_GRAD, MIDDLE_GRAD, ATTENTION_LOW, QUERY_GRAD, SUMS, SPREAD, GROUP,
 LINEAR, INPUT_GRAD, SHARE, BESIDE, PASSED, BELOW, TOTAL) = range(31)
DOWN_SHARE, GATE_SHARE, UP_SHARE, LINEAR_SHARE = range(4)


def dot(a, b, dims=(((1,), (0,)), ((), ()))):
    return lax.dot_general(a, b, dims, preferred_element_type=FULL)


def angles(places, width):
    half = width // 2
    frequency = jnp.power(THETA, -2.0 * jnp.arange(half, dtype=FULL) / width)
    turned = places.astype(FULL)[:, None] * frequency[None, :]
    return (jnp.cos(turned), jnp.sin(turned))


def gather(weight):
    return lax.all_gather(weight, ROWS, axis=0, tiled=True)


def scatter(grad):
    return lax.psum_scatter(grad, ROWS, scatter_dimension=0, tiled=True)


def hop_by(array, hop, seqs):
    return lax.ppermute(array, "seq", [(i, i + hop) for i in range(seqs - hop)])


def hop_back(array, hop, seqs):
    return lax.ppermute(array, "seq", [(i + hop, i) for i in range(seqs - hop)])


def cut(array, pieces):
    size = array.shape[0] // pieces
    return [array[i * size : (i + 1) * size] for i in range(pieces)]


def fetch_window(own, reach, seqs, later):
    if seqs != 4 or reach != 2:
        return [hop_by(own, hop, seqs) for hop in range(reach, 0, -1)]
    near, far = [], []
    last = lax.axis_index("seq") == 2
    pieces = cut(own, 4)
    pieces[3] = lax.optimization_barrier((pieces[3], later()))[0]
    for piece in pieces:
        beside = lax.ppermute(piece, "seq", [(0, 1), (2, 3)])
        below = lax.ppermute(piece, "seq", [(0, 2), (1, 3)])
        passed = lax.ppermute(below, "seq", [(3, 2)])
        near.append((beside, passed))
        far.append(below)
    return [far, [jnp.where(last, passed, beside) for beside, passed in near]]


class Schedule:
    def __init__(self, token, count):
        self.count = count
        self.token = token
        self.values = {}
        self.ready = {}
        self.jobs = []
        self.lines = [[], []]
        self.entered = []
        self.stages = [[None, None, None], [None, None, None]]
        self.now = 0
        self.late = []

    def job(self, cost, needs, work):
        self.jobs.append((cost, needs, work))

    def enter(self, name, halves):
        self.entered.append((name, halves))

    def after(self, *arrays):
        return lax.optimization_barrier((arrays, self.token))[0]

    def barrier(self, *arrays):
        self.token, arrays = lax.optimization_barrier((self.token, arrays))
        return arrays

    def move(self, half, arrived):
        inward, across, outward = (
            None if item is None else (item[0],) + tuple(two) for item, two in zip(self.stages[half], arrived)
        )
        moved = [None, None, None]
        if self.lines[half]:
            name, part = self.lines[half].pop(0)
            moved[0] = (name, part, lax.ppermute(part, LINE, [(0, 1), (3, 2)]))
        pairs = [item[1:] for item in (inward, across) if item is not None]
        sums = list(pair_sums(pairs)) if pairs and pairs[0][0].shape == pairs[-1][0].shape else [
            pair_sums([pair])[0] for pair in pairs]
        if inward is not None:
            pair = sums.pop(0)
            moved[1] = (inward[0], pair, lax.ppermute(pair, LINE, [(1, 2), (2, 1)]))
        if across is not None:
            total = sums.pop(0)
            moved[2] = (across[0], total, lax.ppermute(total, LINE, [(1, 0), (2, 3)]))
        self.stages[half] = moved
        return outward

    def tick(self, budget):
        made, spent, left = {}, 0.0, []
        for cost, needs, work in self.jobs:
            fits = spent == 0.0 or spent + cost <= budget
            if fits and all(self.ready.get(need, self.now + 1) <= self.now for need in needs):
                made.update(work())
                spent += cost
            else:
                left.append((cost, needs, work))
        self.jobs = left
        late = [item for item in self.late if item[1] <= self.now]
        self.late = [item for item in self.late if item[1] > self.now]
        entered, self.entered = self.entered, []
        waiting = [[None if item is None else item[1:] for item in stages] for stages in self.stages]
        made, halves, brought, first = self.barrier(
            made, [item[1] for item in entered], [item[2] for item in late], waiting[0]
        )
        for (name, ignored), (one, two) in zip(entered, halves):
            self.lines[0].append((name, one))
            self.lines[1].append((name, two))
        one = self.move(0, first)
        (second,) = self.barrier(waiting[1])
        two = self.move(1, second)
        if one is not None:
            made[one[0]] = one[1:] + two[1:]
        for item, value in zip(late, brought):
            made[item[0]] = value
        self.now += 1
        for name, value in made.items():
            self.values[name] = value
            self.ready[name] = self.now

    def run(self):
        while self.jobs or self.late or any(self.lines) or any(any(stages) for stages in self.stages):
            self.tick(FINE_BUDGET if self.ready.get((SUMS, self.count), self.now + 1) <= self.now else BUDGET)


def per_device(
    inputs,
    positions,
    query_weight,
    key_weight,
    value_weight,
    output_weight,
    gate_weight,
    up_weight,
    down_weight,
    pre_attention,
    post_attention,
    pre_feedforward,
    post_feedforward,
    cotangent,
):
    hidden = inputs[0]
    upstream = cotangent[0]
    places = positions[0]
    rows, features = hidden.shape
    chunk = min(CHUNK, rows)
    count = rows // chunk
    fine = min(FINE, chunk)
    fines = rows // fine
    split = chunk // fine
    seqs = lax.axis_size("seq")
    reach = min((WINDOW + rows - 2) // rows, seqs - 1)
    heads_width = query_weight.shape[1]
    group_width = key_weight.shape[1]

    gains = jnp.stack([pre_attention, post_attention, pre_feedforward, post_feedforward], axis=1)
    gains = jnp.pad(gains, ((0, 0), (0, 124)))
    packed = gather(jnp.concatenate([key_weight, value_weight, gains], axis=1))
    group_full = packed[:, : 2 * group_width]
    gains = 1.0 + packed[:, 2 * group_width : 2 * group_width + 4].astype(FULL).T
    query_weight, output_weight, packed = lax.optimization_barrier((query_weight, output_weight, packed))
    query_full = gather(query_weight)
    output_full = gather(output_weight)

    cosine, sine = angles(places, HD)
    normed_one, own, factor = project_group(hidden, gains[:1], group_full, cosine, sine)
    query_low = project_heads(normed_one, query_full, cosine, sine)
    fetched = fetch_window(own, reach, seqs, lambda: query_low)
    low, bounds = limits(places, chunk)
    low_wide = jnp.broadcast_to(low[:, None], (rows, 128))
    low_row = low[None, :]
    fetched, query_low, low_wide, low_row, bounds, gate_weight, up_weight, down_weight = lax.optimization_barrier(
        (fetched, query_low, low_wide, low_row, bounds, gate_weight, up_weight, down_weight)
    )
    blocks = []
    for block in fetched:
        blocks += block if isinstance(block, list) else [block]
    blocks += cut(own, rows // blocks[0].shape[0])
    gate_full = gather(gate_weight)
    up_full = gather(up_weight)
    down_full = gather(down_weight)

    place = lax.axis_index(LINE)
    middle = ((place == 1) | (place == 2)).astype(jnp.int32)[None]
    plan = Schedule(bounds[0, 0], count)
    values = plan.values

    def part(array, index, size=chunk):
        return array[index * size : (index + 1) * size]

    def every(kind, number):
        return [values[kind, i] for i in range(number)]

    def attend_job(i):
        def work():
            (query,) = plan.after(query_low)
            head, stat = attend(query, blocks, low_wide, bounds, i, 1, chunk)
            plan.enter((ATTENDED, i), back_out([(head, output_full)], chunk // 2))
            return {(HEADS, i): head, (STAT, i): stat}

        plan.job(12.0 if i else 40.0, [], work)

    def forward_job(i):
        def work():
            kinds = (ATTENDED, BETWEEN, NORMED, GATE, UP, MIXED)
            made = gate_call(middle, values[ATTENDED, i], hidden, gains, gate_full, up_full, i)
            plan.enter((FED, i), back_out([(made[5], down_full)], chunk // 2))
            return {(kind, i): array for kind, array in zip(kinds, made)}

        plan.job(36.0, [(ATTENDED, i)], work)

    def backward_job(i):
        def work():
            kinds = (RESULT, FED_LOW, GAIN_FOUR, GATE_LOW, UP_LOW)
            made = mixed_back(
                middle, values[FED, i], values[BETWEEN, i], upstream, gains, down_full,
                values[GATE, i], values[UP, i], i, values.get((RESULT, 0)),
            )
            values[RESULT, 0] = made[0]
            plan.enter((NORMED_GRAD, i), back_out([(made[3], gate_full), (made[4], up_full)], chunk // 2))
            return {(kind, i): array for kind, array in zip(kinds[1:], made[1:])}

        plan.job(40.0, [(FED, i)], work)

    def attention_job(i):
        def work():
            kinds = (MIDDLE_GRAD, ATTENTION_LOW, GAIN_TWO, GAIN_THREE)
            *made, heads_grad = attention_low(
                middle, values[NORMED_GRAD, i], values[BETWEEN, i], values[ATTENDED, i], upstream, gains, output_full, i
            )
            query_grad, *sums = attend_back(
                query_low, heads_grad, values[HEADS, i], values[STAT, i], blocks, low_row,
                cosine, sine, bounds, values.get((SUMS, i)), i, 1, chunk, sent if i == count - 1 else (),
            )
            made = {(kind, i): array for kind, array in zip(kinds, made)}
            made.update({(QUERY_GRAD, i): query_grad, (SUMS, i + 1): sums[-1]})
            made.update({(SPREAD, k): array for k, array in enumerate(sums[:-1])})
            return made

        plan.job(44.0, [(NORMED_GRAD, i)] + ([(SUMS, i)] if i else []), work)

    def first_spread_job():
        def work():
            for k in range(4):
                near = values[SPREAD, 4 + k]
                beside = lax.ppermute(near, "seq", [(1, 0), (3, 2)])
                passed = lax.ppermute(near, "seq", [(2, 3)])
                plan.late.append(((BESIDE, k), plan.now + k // 2 + 1, beside))
                plan.late.append(((PASSED, k), plan.now + k // 2, passed))
            return {}

        plan.job(1.0, [(SUMS, count)], work)

    def second_spread_job(k):
        def work():
            (below,) = pair_sums([(values[SPREAD, k], values[PASSED, k])])
            plan.late.append(((BELOW, k), plan.now, lax.ppermute(below, "seq", [(2, 0), (3, 1)])))
            return {}

        plan.job(1.0, [(PASSED, k)], work)

    def hops_job():
        def work():
            for hop in range(1, reach + 1):
                plan.late.append(((BESIDE, hop), plan.now + 1, hop_back(values[SPREAD, reach - hop], hop, seqs)))
            return {}

        plan.job(1.0, [(SUMS, count)], work)

    def group_job(k, needs):
        def work():
            arrived = [values[need] for need in needs]
            group = finish_group(values[SUMS, count], arrived, cosine, sine, k)
            made = {(GROUP, k): group}
            each = fines // groups
            for i in range(k * each, (k + 1) * each):
                *halves, made[GAIN_ONE, i] = linear_back(
                    values[QUERY_GRAD, i // split], i % split, group, i - k * each, query_full, group_full,
                    hidden, factor, i, fine,
                )
                plan.enter((LINEAR, i), halves)
            return made

        plan.job(3.0 + 5.0 * fines // groups, needs, work)

    def input_job(i):
        def work():
            values[INPUT_GRAD, 0] = input_grad(
                middle, values[LINEAR, i], hidden, values[MIDDLE_GRAD, i // split], i % split, gains, i,
                values.get((INPUT_GRAD, 0)),
            )
            return {}

        plan.job(4.0, [(LINEAR, i)], work)

    def share_job(index, cost, needs, left, right):
        def work():
            lefts = left()
            lefts[0], = plan.after(lefts[0])
            return {(SHARE, index): share_call(lefts, right())}

        plan.job(cost, needs, work)

    def scatter_job(index, ticks, needs):
        def work():
            (share,) = plan.after(values[SHARE, index])
            plan.late.append(((TOTAL, index), plan.now + ticks - 1, scatter(share)))
            return {}

        plan.job(0.0, [(SHARE, index)] + needs, work)

    def linear_share_job():
        def work():
            kinds = ((GAIN_ONE, fines), (GAIN_TWO, count), (GAIN_THREE, count), (GAIN_FOUR, count))
            columns = jnp.stack([jnp.sum(sum(every(*kind)), axis=0) for kind in kinds], axis=1)
            columns = jnp.pad(columns.astype(LOW), ((0, 0), (0, 124)))
            (left,) = plan.after(normed_one)
            grads = [share_call([left], every(QUERY_GRAD, count)), share_call([left], every(GROUP, groups))]
            grads.append(share_call(every(ATTENTION_LOW, count), every(HEADS, count)))
            return {(SHARE, LINEAR_SHARE): jnp.concatenate(grads + [columns], axis=1)}

        plan.job(30.0, [(GAIN_ONE, i) for i in range(fines)], work)

    square = seqs == 4 and reach == 2
    groups = 4 if square else 1
    sent = (rows // 4,) * 8 if square else (rows,) * reach
    for i in range(count):
        attend_job(i)
    for i in range(count):
        forward_job(i)
    for i in range(count):
        backward_job(i)
    for i in range(count):
        attention_job(i)
    if square:
        first_spread_job()
        for k in range(4):
            second_spread_job(k)
        for k in range(4):
            group_job(k, [(BESIDE, k), (BELOW, k)])
    else:
        hops_job()
        group_job(0, [(BESIDE, hop) for hop in range(1, reach + 1)])
    backs = [(GATE_LOW, i) for i in range(count)] + [(SUMS, count)]
    share_job(DOWN_SHARE, 26.0, backs, lambda: every(FED_LOW, count), lambda: every(MIXED, count))
    share_job(GATE_SHARE, 26.0, backs, lambda: every(NORMED, count), lambda: every(GATE_LOW, count))
    share_job(UP_SHARE, 26.0, backs, lambda: every(NORMED, count), lambda: every(UP_LOW, count))
    linear_share_job()
    scatter_job(DOWN_SHARE, 3, [(GROUP, 0)] if groups == 1 else [(BELOW, 1)])
    scatter_job(GATE_SHARE, 3, [(TOTAL, DOWN_SHARE)])
    scatter_job(UP_SHARE, 3, [(TOTAL, GATE_SHARE)])
    scatter_job(LINEAR_SHARE, 2, [(TOTAL, UP_SHARE)])
    for i in range(fines):
        input_job(i)
    plan.run()

    shares = [array.astype(FULL) for array in every(TOTAL, 4)]
    linear_share = shares[LINEAR_SHARE]
    width = heads_width + 2 * group_width
    gain_grads = linear_share[:, width + heads_width :][:, :4].T
    gain_one = gain_grads[0]
    for turn in (1, 2):
        gain_one = gain_one + lax.ppermute(gain_one, LINE, [(i, i ^ turn) for i in range(4)])
    return (
        values[RESULT, 0][None],
        values[INPUT_GRAD, 0][None],
        linear_share[:, :heads_width],
        linear_share[:, heads_width : heads_width + group_width],
        linear_share[:, heads_width + group_width : width],
        linear_share[:, width : width + heads_width],
        shares[GATE_SHARE],
        shares[UP_SHARE],
        shares[DOWN_SHARE],
        gain_one,
        gain_grads[1],
        gain_grads[2],
        gain_grads[3],
    )


def solution(mesh):
    tokens = P("dp", "seq", None)
    weight = P(ROWS, LINE)
    gain = P(ROWS)
    return jax.shard_map(
        per_device,
        mesh=mesh,
        in_specs=(tokens, P("dp", "seq")) + (weight,) * 7 + (gain,) * 4 + (tokens,),
        out_specs=(tokens, tokens) + (weight,) * 7 + (gain,) * 4,
        check_vma=False,
    )
```

```python
import functools

import jax
import jax.numpy as jnp
from jax import lax
from jax.experimental import pallas as pl
from jax.experimental.pallas import tpu as pltpu
from jax.sharding import PartitionSpec as P

HD = 256
WINDOW = 4096
CAP = 50
EPS = 1e-06
KEYS = 512
LOG2E = 1.4426950408889634
BEND = HD ** (-0.5) / CAP
RAISE = CAP * LOG2E
GELU = 0.7978845608028654
NT = (((1,), (1,)), ((), ()))
TN = (((0,), (0,)), ((), ()))
SMALL = pl.CostEstimate(flops=1, bytes_accessed=1, transcendentals=0)


def rotate(values, cosine, sine):
    half = HD // 2
    first, second = values[:, :half], values[:, half:]
    return jnp.concatenate([first * cosine - second * sine, second * cosine + first * sine], axis=1)


def stack_heads(block):
    return jnp.concatenate([block[:, :HD], block[:, HD:]], axis=0)


def load_pieces(pieces, window_ref, sems):
    rows = pieces[0].shape[0]
    copies = [
        pltpu.make_async_copy(piece, window_ref.at[pl.ds(i * rows, rows)], sems.at[i]) for i, piece in enumerate(pieces)
    ]
    for copy in copies:
        copy.start()
    for copy in copies:
        copy.wait()


def attend_kernel(first, number, bounds_ref, query_ref, low_ref, *rest):
    pieces, (heads_ref, stat_ref, acc_ref, sum_ref, window_ref, sems) = rest[:number], rest[number:]
    step = pl.program_id(0)

    @pl.when(step == 0)
    def _():
        load_pieces(pieces, window_ref, sems)

    chunk = query_ref.shape[0]
    base = (first + step) * chunk
    query = stack_heads(query_ref[...])
    acc_ref[...] = jnp.zeros_like(acc_ref)
    sum_ref[...] = jnp.zeros_like(sum_ref)

    def add_block(offset, size, masked, causal):
        rows = pl.ds(pl.multiple_of(base + offset, 256), size)
        keys = window_ref[rows, :HD]
        values = window_ref[rows, HD:]
        scores = lax.dot_general(query, keys, NT, preferred_element_type=jnp.float32)
        raised = jnp.exp2(jnp.tanh(scores * BEND) * RAISE)
        if masked:
            column = offset + lax.broadcasted_iota(jnp.int32, (chunk, size), 1)
            keep = column >= jnp.concatenate([low_ref[...]] * (size // 128), axis=1)
            if causal:
                keep &= column <= WINDOW + lax.broadcasted_iota(jnp.int32, (chunk, size), 0)
            raised = jnp.where(jnp.concatenate([keep, keep], axis=0), raised, 0.0)
        part = raised[:, :128]
        for lane in range(128, size, 128):
            part = part + raised[:, lane : lane + 128]
        sum_ref[...] += part
        acc_ref[...] += jnp.dot(raised.astype(jnp.bfloat16), values, preferred_element_type=jnp.float32)

    def masked_step(block, carry):
        add_block(block * KEYS, KEYS, True, False)
        return carry

    def full_step(block, carry):
        add_block(block * KEYS, KEYS, False, False)
        return carry

    blocks = WINDOW // KEYS
    lax.fori_loop(bounds_ref[first + step, 0], bounds_ref[first + step, 1], masked_step, 0)
    lax.fori_loop(bounds_ref[first + step, 1], blocks, full_step, 0)
    add_block(WINDOW, chunk, True, True)
    total = jnp.sum(sum_ref[...], axis=1, keepdims=True)
    heads = (acc_ref[...] / total).astype(jnp.bfloat16)
    heads_ref[:, :HD] = heads[:chunk]
    heads_ref[:, HD:] = heads[chunk:]
    stat_ref[...] = jnp.broadcast_to(jnp.log2(total), stat_ref.shape)


def attend(query, pieces, low, bounds, first, count, chunk):
    rows = count * chunk
    span = len(pieces) * pieces[0].shape[0]
    return pl.pallas_call(
        functools.partial(attend_kernel, first, len(pieces)),
        out_shape=(
            jax.ShapeDtypeStruct((rows, 2 * HD), jnp.bfloat16),
            jax.ShapeDtypeStruct((2 * rows, 128), jnp.float32),
        ),
        grid_spec=pltpu.PrefetchScalarGridSpec(
            num_scalar_prefetch=1,
            grid=(count,),
            in_specs=[
                pl.BlockSpec((chunk, 2 * HD), lambda g, b: (first + g, 0)),
                pl.BlockSpec((chunk, 128), lambda g, b: (first + g, 0)),
            ]
            + [pl.BlockSpec(memory_space=pl.ANY)] * len(pieces),
            out_specs=[
                pl.BlockSpec((chunk, 2 * HD), lambda g, b: (g, 0)),
                pl.BlockSpec((2 * chunk, 128), lambda g, b: (g, 0)),
            ],
            scratch_shapes=[
                pltpu.VMEM((2 * chunk, HD), jnp.float32),
                pltpu.VMEM((2 * chunk, 128), jnp.float32),
                pltpu.VMEM((span, 2 * HD), jnp.bfloat16),
                pltpu.SemaphoreType.DMA((len(pieces),)),
            ],
        ),
        compiler_params=pltpu.CompilerParams(vmem_limit_bytes=48 * 2**20),
        cost_estimate=SMALL,
        name="attend",
    )(bounds, query, low, *pieces)


def attend_back_kernel(
    first, number, carried, sent, bounds_ref, query_ref, grad_ref, heads_ref, stat_ref, low_ref, cosine_ref, sine_ref, *rest
):
    pieces, rest = rest[:number], rest[number:]
    if carried:
        before_ref, *rest = rest
    dquery_ref, *afters, sum_ref, acc_ref, window_ref, sem, sems = rest
    step = pl.program_id(0)
    chunk = query_ref.shape[0]
    base = (first + step) * chunk

    @pl.when(step == 0)
    def _():
        if carried:
            copy = pltpu.make_async_copy(before_ref, sum_ref, sem)
            copy.start()
        else:
            sum_ref[...] = jnp.zeros_like(sum_ref)
        load_pieces(pieces, window_ref, sems)
        if carried:
            copy.wait()

    query = stack_heads(query_ref[...])
    grad = stack_heads(grad_ref[...])
    heads = stack_heads(heads_ref[...])
    inner = jnp.sum(grad.astype(jnp.float32) * heads.astype(jnp.float32), axis=1, keepdims=True)
    inner = jnp.broadcast_to(inner, (2 * chunk, 128)).T[:1]
    stat = stat_ref[...].T[:1]
    low = low_ref[...]
    low = jnp.concatenate([low, low], axis=1)
    acc_ref[...] = jnp.zeros_like(acc_ref)

    def add_block(offset, size, masked, causal):
        place = pl.multiple_of(base + offset, 256)
        rows = pl.ds(place, size)
        keys = window_ref[rows, :HD]
        values = window_ref[rows, HD:]
        scores = lax.dot_general(keys, query, NT, preferred_element_type=jnp.float32)
        slope = jnp.tanh(scores * BEND)
        shares = jnp.exp2(slope * RAISE - stat)
        if masked:
            row = offset + lax.broadcasted_iota(jnp.int32, (size, 2 * chunk), 0)
            keep = row >= low
            if causal:
                column = lax.broadcasted_iota(jnp.int32, (size, chunk), 1)
                keep &= row <= WINDOW + jnp.concatenate([column, column], axis=1)
            shares = jnp.where(keep, shares, 0.0)
        share_grad = lax.dot_general(values, grad, NT, preferred_element_type=jnp.float32)
        score_low = (shares * (share_grad - inner) * (1.0 - slope * slope)).astype(jnp.bfloat16)
        sum_ref[rows, HD:] += jnp.dot(shares.astype(jnp.bfloat16), grad, preferred_element_type=jnp.float32)
        sum_ref[rows, :HD] += jnp.dot(score_low, query, preferred_element_type=jnp.float32)
        acc_ref[...] += lax.dot_general(keys, score_low, TN, preferred_element_type=jnp.float32)

    def masked_step(block, carry):
        add_block(block * KEYS, KEYS, True, False)
        return carry

    def full_step(block, carry):
        add_block(block * KEYS, KEYS, False, False)
        return carry

    blocks = WINDOW // KEYS
    lax.fori_loop(bounds_ref[first + step, 0], bounds_ref[first + step, 1], masked_step, 0)
    lax.fori_loop(bounds_ref[first + step, 1], blocks, full_step, 0)
    add_block(WINDOW, chunk, True, True)
    dquery = (acc_ref[...].T * HD ** (-0.5)).astype(jnp.bfloat16).astype(jnp.float32)
    for head in range(2):
        turned = rotate(dquery[head * chunk : (head + 1) * chunk], cosine_ref[...], -sine_ref[...])
        dquery_ref[:, head * HD : (head + 1) * HD] = turned.astype(jnp.bfloat16)

    @pl.when(step == pl.num_programs(0) - 1)
    def _():
        done = 0
        for out in afters[:-1]:
            out[...] = sum_ref[done : done + out.shape[0], :].astype(jnp.bfloat16)
            done += out.shape[0]
        copy = pltpu.make_async_copy(sum_ref.at[pl.ds(done, sum_ref.shape[0] - done)], afters[-1], sem)
        copy.start()
        copy.wait()


def attend_back(query, grad, heads, stat, pieces, low_row, cosine, sine, bounds, before, first, count, chunk,
                sent):
    rows = count * chunk
    span = len(pieces) * pieces[0].shape[0]
    carried = before is not None
    extra = [before] if carried else []
    return pl.pallas_call(
        functools.partial(attend_back_kernel, first, len(pieces), carried, sent),
        out_shape=(
            jax.ShapeDtypeStruct((rows, 2 * HD), jnp.bfloat16),
            *(jax.ShapeDtypeStruct((size, 2 * HD), jnp.bfloat16) for size in sent),
            jax.ShapeDtypeStruct((span - sum(sent), 2 * HD), jnp.float32),
        ),
        grid_spec=pltpu.PrefetchScalarGridSpec(
            num_scalar_prefetch=1,
            grid=(count,),
            in_specs=[
                pl.BlockSpec((chunk, 2 * HD), lambda g, b: (first + g, 0)),
                pl.BlockSpec((chunk, 2 * HD), lambda g, b: (g, 0)),
                pl.BlockSpec((chunk, 2 * HD), lambda g, b: (g, 0)),
                pl.BlockSpec((2 * chunk, 128), lambda g, b: (g, 0)),
                pl.BlockSpec((1, chunk), lambda g, b: (0, first + g)),
                pl.BlockSpec((chunk, HD // 2), lambda g, b: (first + g, 0)),
                pl.BlockSpec((chunk, HD // 2), lambda g, b: (first + g, 0)),
            ]
            + [pl.BlockSpec(memory_space=pl.ANY)] * (len(pieces) + len(extra)),
            out_specs=[
                pl.BlockSpec((chunk, 2 * HD), lambda g, b: (g, 0)),
                *(pl.BlockSpec((size, 2 * HD), lambda g, b: (0, 0)) for size in sent),
                pl.BlockSpec(memory_space=pl.ANY),
            ],
            scratch_shapes=[
                pltpu.VMEM((span, 2 * HD), jnp.float32),
                pltpu.VMEM((HD, 2 * chunk), jnp.float32),
                pltpu.VMEM((span, 2 * HD), jnp.bfloat16),
                pltpu.SemaphoreType.DMA,
                pltpu.SemaphoreType.DMA((len(pieces),)),
            ],
        ),
        compiler_params=pltpu.CompilerParams(vmem_limit_bytes=60 * 2**20),
        cost_estimate=SMALL,
        name="attend_back",
    )(bounds, query, grad, heads, stat, low_row, cosine, sine, *pieces, *extra)


def limits(places, chunk):
    count = places.shape[0] // chunk
    low = WINDOW + jnp.arange(chunk, dtype=jnp.int32)[None, :] - jnp.minimum(places.reshape(count, chunk), WINDOW - 1)
    blocks = WINDOW // KEYS
    begin = jnp.minimum(jnp.min(low, axis=1) // KEYS, blocks)
    full = jnp.minimum((jnp.max(low, axis=1) + KEYS - 1) // KEYS, blocks)
    return low.reshape(-1), jnp.stack([begin, full], axis=1)


def scaled(values):
    factor = lax.rsqrt(jnp.mean(values * values, axis=-1, keepdims=True) + EPS)
    return factor, values * factor


def project_group_kernel(hidden_ref, gain_ref, weight_ref, cosine_ref, sine_ref, normed_ref, own_ref, factor_ref):
    factor, normed = scaled(hidden_ref[...].astype(jnp.float32))
    factor_ref[...] = jnp.broadcast_to(factor, factor_ref.shape)
    normed = (normed * gain_ref[...]).astype(jnp.bfloat16)
    normed_ref[...] = normed
    linear = jnp.dot(normed, weight_ref[...], preferred_element_type=jnp.float32)
    own_ref[:, :HD] = rotate(linear[:, :HD], cosine_ref[...], sine_ref[...]).astype(jnp.bfloat16)
    own_ref[:, HD:] = linear[:, HD:].astype(jnp.bfloat16)


def project_group(hidden, gain, weight, cosine, sine):
    rows, features = hidden.shape
    tile = min(256, rows)
    return pl.pallas_call(
        project_group_kernel,
        out_shape=(
            jax.ShapeDtypeStruct((rows, features), jnp.bfloat16),
            jax.ShapeDtypeStruct((rows, 2 * HD), jnp.bfloat16),
            jax.ShapeDtypeStruct((rows, 128), jnp.float32),
        ),
        grid=(rows // tile,),
        in_specs=[
            pl.BlockSpec((tile, features), lambda g: (g, 0)),
            pl.BlockSpec((1, features), lambda g: (0, 0)),
            pl.BlockSpec((features, 2 * HD), lambda g: (0, 0), pipeline_mode=pl.Buffered(1)),
            pl.BlockSpec((tile, HD // 2), lambda g: (g, 0)),
            pl.BlockSpec((tile, HD // 2), lambda g: (g, 0)),
        ],
        out_specs=[
            pl.BlockSpec((tile, features), lambda g: (g, 0)),
            pl.BlockSpec((tile, 2 * HD), lambda g: (g, 0)),
            pl.BlockSpec((tile, 128), lambda g: (g, 0)),
        ],
        compiler_params=pltpu.CompilerParams(vmem_limit_bytes=32 * 2**20),
        cost_estimate=SMALL,
        name="project_group",
    )(hidden, gain, weight, cosine, sine)


def project_heads_kernel(normed_ref, weight_ref, cosine_ref, sine_ref, query_ref):
    linear = jnp.dot(normed_ref[...], weight_ref[...], preferred_element_type=jnp.float32)
    for head in range(0, 2 * HD, HD):
        turned = rotate(linear[:, head : head + HD], cosine_ref[...], sine_ref[...])
        query_ref[:, head : head + HD] = turned.astype(jnp.bfloat16)


def project_heads(normed, weight, cosine, sine):
    rows, features = normed.shape
    tile = min(256, rows)
    return pl.pallas_call(
        project_heads_kernel,
        out_shape=jax.ShapeDtypeStruct((rows, 2 * HD), jnp.bfloat16),
        grid=(rows // tile,),
        in_specs=[
            pl.BlockSpec((tile, features), lambda g: (g, 0)),
            pl.BlockSpec((features, 2 * HD), lambda g: (0, 0), pipeline_mode=pl.Buffered(1)),
            pl.BlockSpec((tile, HD // 2), lambda g: (g, 0)),
            pl.BlockSpec((tile, HD // 2), lambda g: (g, 0)),
        ],
        out_specs=pl.BlockSpec((tile, 2 * HD), lambda g: (g, 0)),
        compiler_params=pltpu.CompilerParams(vmem_limit_bytes=32 * 2**20),
        cost_estimate=SMALL,
        name="project_heads",
    )(normed, weight, cosine, sine)


def finish_group_kernel(cosine_ref, sine_ref, own_ref, *rest):
    *arrived, low_ref = rest
    total = own_ref[...]
    for block in arrived:
        total = total + block[...].astype(jnp.float32)
    key_rot = (total[:, :HD] * HD ** (-0.5)).astype(jnp.bfloat16).astype(jnp.float32)
    low_ref[:, :HD] = rotate(key_rot, cosine_ref[...], -sine_ref[...]).astype(jnp.bfloat16)
    low_ref[:, HD:] = total[:, HD:].astype(jnp.bfloat16)


def finish_group(sums, arrived, cosine, sine, index):
    rows = arrived[0].shape[0]
    tile = min(256, rows)
    skip = index * (rows // tile)
    wide = pl.BlockSpec((tile, 2 * HD), lambda g: (g, 0))
    half = pl.BlockSpec((tile, HD // 2), lambda g: (skip + g, 0))
    return pl.pallas_call(
        finish_group_kernel,
        out_shape=jax.ShapeDtypeStruct((rows, 2 * HD), jnp.bfloat16),
        grid=(rows // tile,),
        in_specs=[half, half, pl.BlockSpec((tile, 2 * HD), lambda g: (skip + g, 0))] + [wide] * len(arrived),
        out_specs=wide,
        cost_estimate=SMALL,
        name="finish_group",
    )(cosine, sine, sums, *arrived)


ROW = 64
TILE = 256
WIDE = 768
GATE_TILE = 384


def pick(middle, total_ref, outward_ref, rows):
    total = jnp.where(middle, total_ref[rows, :].astype(jnp.float32), outward_ref[rows, :].astype(jnp.float32))
    return total


def fold(values):
    return jnp.sum(values.reshape(-1, 8, values.shape[1]), axis=0)


def gate_kernel(number, chunk, middle_ref, *rest):
    came, rest = rest[: 2 * number], rest[2 * number :]
    hidden_ref, gains_ref, gate_weight_ref, up_weight_ref, *rest = rest
    attended_ref, between_ref, normed_ref, gate_ref, up_ref, mixed_ref = rest
    middle = middle_ref[0] == 1

    @pl.when(pl.program_id(0) == 0)
    def _():
        for i in range(number):

            def step(r, carry):
                rows = pl.ds(pl.multiple_of(r * ROW, ROW), ROW)
                place = pl.ds(pl.multiple_of(i * chunk + r * ROW, ROW), ROW)
                attended = pick(middle, came[2 * i], came[2 * i + 1], rows)
                between = hidden_ref[place, :].astype(jnp.float32) + scaled(attended)[1] * gains_ref[1:2, :]
                attended_ref[place, :] = attended.astype(jnp.bfloat16)
                between_ref[place, :] = between
                normed_ref[place, :] = (scaled(between)[1] * gains_ref[2:3, :]).astype(jnp.bfloat16)
                return carry

            lax.fori_loop(0, chunk // ROW, step, 0)

    gate = jnp.dot(normed_ref[...], gate_weight_ref[...], preferred_element_type=jnp.float32)
    up = jnp.dot(normed_ref[...], up_weight_ref[...], preferred_element_type=jnp.float32)
    gate_ref[...] = gate
    up_ref[...] = up
    mixed_ref[...] = (jax.nn.gelu(gate, approximate=True) * up).astype(jnp.bfloat16)


def full_block(rows, columns):
    return pl.BlockSpec((rows, columns), lambda n, m: (0, 0))


def gate_call(middle, came, hidden, gains, gate_weight, up_weight, pair):
    number = len(came) // 2
    chunk, features = came[0].shape
    rows = number * chunk
    units = gate_weight.shape[1]
    wide = pl.BlockSpec((features, GATE_TILE), lambda n, m: (0, n))
    tall = pl.BlockSpec((rows, GATE_TILE), lambda n, m: (0, n))
    return pl.pallas_call(
        functools.partial(gate_kernel, number, chunk),
        out_shape=(
            jax.ShapeDtypeStruct((rows, features), jnp.bfloat16),
            jax.ShapeDtypeStruct((rows, features), jnp.float32),
            jax.ShapeDtypeStruct((rows, features), jnp.bfloat16),
            jax.ShapeDtypeStruct((rows, units), jnp.float32),
            jax.ShapeDtypeStruct((rows, units), jnp.float32),
            jax.ShapeDtypeStruct((rows, units), jnp.bfloat16),
        ),
        grid_spec=pltpu.PrefetchScalarGridSpec(
            num_scalar_prefetch=1,
            grid=(units // GATE_TILE,),
            in_specs=[full_block(chunk, features)] * len(came)
            + [pl.BlockSpec((rows, features), lambda n, m: (pair, 0)), full_block(4, features), wide, wide],
            out_specs=[full_block(rows, features)] * 3 + [tall] * 3,
        ),
        compiler_params=pltpu.CompilerParams(vmem_limit_bytes=60 * 2**20),
        cost_estimate=SMALL,
        name="gate",
    )(middle, *came, hidden, gains, gate_weight, up_weight)


def back_out_kernel(number, chunk, *rest):
    terms, outs = rest[:-number], rest[-number:]
    total = 0.0
    for left, weight in zip(terms[::2], terms[1::2]):
        total = total + lax.dot_general(left[...], weight[...], NT, preferred_element_type=jnp.float32)
    total = total.astype(jnp.bfloat16)
    for i, out in enumerate(outs):
        out[...] = total[i * chunk : (i + 1) * chunk]


def back_out(terms, chunk):
    rows, units = terms[0][0].shape
    features = terms[0][1].shape[0]
    number = rows // chunk
    left = pl.BlockSpec((rows, units), lambda n: (0, 0))
    weight = pl.BlockSpec((WIDE, units), lambda n: (n, 0))
    return pl.pallas_call(
        functools.partial(back_out_kernel, number, chunk),
        out_shape=[jax.ShapeDtypeStruct((chunk, features), jnp.bfloat16)] * number,
        grid=(features // WIDE,),
        in_specs=[left, weight] * len(terms),
        out_specs=[pl.BlockSpec((chunk, WIDE), lambda n: (0, n))] * number,
        compiler_params=pltpu.CompilerParams(vmem_limit_bytes=48 * 2**20),
        cost_estimate=SMALL,
        name="back_out",
    )(*[array for term in terms for array in term])


def mixed_back_kernel(number, chunk, middle_ref, *rest):
    came, rest = rest[: 2 * number], rest[2 * number :]
    between_ref, upstream_ref, gains_ref, down_ref, gate_ref, up_ref, *rest = rest
    result_ref, fed_ref, gain_ref, gate_low_ref, up_low_ref = rest[-5:]
    middle = middle_ref[0] == 1

    @pl.when(pl.program_id(0) == 0)
    def _():
        gain_ref[...] = jnp.zeros_like(gain_ref)
        for i in range(number):

            def step(r, carry):
                rows = pl.ds(pl.multiple_of(r * ROW, ROW), ROW)
                place = pl.ds(pl.multiple_of(i * chunk + r * ROW, ROW), ROW)
                factor, normed = scaled(pick(middle, came[2 * i], came[2 * i + 1], rows))
                raised = normed * gains_ref[3:4, :]
                result_ref[place, :] = (between_ref[place, :] + raised).astype(jnp.bfloat16)
                given = upstream_ref[place, :].astype(jnp.float32)
                gain_ref[...] += fold(given * normed)
                inner = jnp.mean(given * raised, axis=-1, keepdims=True)
                fed_ref[place, :] = (factor * (given * gains_ref[3:4, :] - normed * inner)).astype(jnp.bfloat16)
                return carry

            lax.fori_loop(0, chunk // ROW, step, 0)

    mixed_grad = jnp.dot(fed_ref[...], down_ref[...], preferred_element_type=jnp.float32)
    gate = gate_ref[...]
    inside = GELU * (gate + 0.044715 * gate * gate * gate)
    bent = jnp.tanh(inside)
    half = 0.5 * (1.0 + bent)
    slope = half + 0.5 * gate * (1.0 - bent * bent) * (GELU * (1.0 + 3 * 0.044715 * gate * gate))
    gate_low_ref[...] = (mixed_grad * up_ref[...] * slope).astype(jnp.bfloat16)
    up_low_ref[...] = (mixed_grad * (gate * half)).astype(jnp.bfloat16)


def mixed_back(middle, came, between, upstream, gains, down_weight, gate, up, pair, before):
    number = len(came) // 2
    chunk, features = came[0].shape
    rows = number * chunk
    units = down_weight.shape[1]
    tall = pl.BlockSpec((rows, GATE_TILE), lambda n, m: (0, n))
    extra = [] if before is None else [before]
    return pl.pallas_call(
        functools.partial(mixed_back_kernel, number, chunk),
        out_shape=(
            jax.ShapeDtypeStruct(upstream.shape, jnp.bfloat16),
            jax.ShapeDtypeStruct((rows, features), jnp.bfloat16),
            jax.ShapeDtypeStruct((8, features), jnp.float32),
            jax.ShapeDtypeStruct((rows, units), jnp.bfloat16),
            jax.ShapeDtypeStruct((rows, units), jnp.bfloat16),
        ),
        grid_spec=pltpu.PrefetchScalarGridSpec(
            num_scalar_prefetch=1,
            grid=(units // GATE_TILE,),
            in_specs=[full_block(chunk, features)] * len(came)
            + [
                full_block(rows, features),
                pl.BlockSpec((rows, features), lambda n, m: (pair, 0)),
                full_block(4, features),
                pl.BlockSpec((features, GATE_TILE), lambda n, m: (0, n)),
                tall,
                tall,
            ]
            + [pl.BlockSpec(memory_space=pl.ANY)] * len(extra),
            out_specs=[pl.BlockSpec((rows, features), lambda n, m: (pair, 0)), full_block(rows, features)]
            + [full_block(8, features)]
            + [tall] * 2,
        ),
        input_output_aliases={} if before is None else {len(came) + 7: 0},
        compiler_params=pltpu.CompilerParams(vmem_limit_bytes=60 * 2**20),
        cost_estimate=SMALL,
        name="mixed_back",
    )(middle, *came, between, upstream, gains, down_weight, gate, up, *extra)


def attention_low_kernel(middle_ref, *rest):
    came, rest = rest[:4], rest[4:]
    (between_ref, attended_ref, upstream_ref, gains_ref, weight_ref,
     grad_ref, low_ref, gain_two_ref, gain_three_ref, heads_ref) = rest
    middle = middle_ref[0] == 1
    step = pl.program_id(0)
    early = step < pl.num_programs(0) // 2
    size = between_ref.shape[0]

    @pl.when(step == 0)
    def _():
        gain_two_ref[...] = jnp.zeros_like(gain_two_ref)
        gain_three_ref[...] = jnp.zeros_like(gain_three_ref)

    rows = pl.ds(0, size)
    total = jnp.where(early, pick(middle, came[0], came[1], rows), pick(middle, came[2], came[3], rows))
    factor, normed = scaled(between_ref[...])
    gain_three_ref[...] += fold(total * normed)
    raised = total * gains_ref[2:3, :]
    inner = jnp.mean(raised * normed, axis=-1, keepdims=True)
    grad = upstream_ref[...].astype(jnp.float32) + factor * (raised - normed * inner)
    grad_ref[...] = grad
    factor, normed = scaled(attended_ref[...].astype(jnp.float32))
    gain_two_ref[...] += fold(grad * normed)
    raised = grad * gains_ref[1:2, :]
    inner = jnp.mean(raised * normed, axis=-1, keepdims=True)
    low_ref[pl.ds(pl.multiple_of(step * size, size), size), :] = (factor * (raised - normed * inner)).astype(jnp.bfloat16)

    @pl.when(step == pl.num_programs(0) - 1)
    def _():
        heads = jnp.dot(low_ref[...], weight_ref[...], preferred_element_type=jnp.float32)
        heads_ref[...] = heads.astype(jnp.bfloat16)


def attention_low(middle, came, between, attended, upstream, gains, weight, index):
    chunk, features = between.shape
    width = weight.shape[1]
    size = ROW
    parts = chunk // size

    def some(offset):
        return pl.BlockSpec((size, features), lambda n, m: (offset * parts + n, 0))

    first = pl.BlockSpec((size, features), lambda n, m: (jnp.minimum(n, parts // 2 - 1), 0))
    second = pl.BlockSpec((size, features), lambda n, m: (jnp.maximum(n - parts // 2, 0), 0))
    return pl.pallas_call(
        attention_low_kernel,
        out_shape=(
            jax.ShapeDtypeStruct((chunk, features), jnp.float32),
            jax.ShapeDtypeStruct((chunk, features), jnp.bfloat16),
            jax.ShapeDtypeStruct((8, features), jnp.float32),
            jax.ShapeDtypeStruct((8, features), jnp.float32),
            jax.ShapeDtypeStruct((chunk, width), jnp.bfloat16),
        ),
        grid_spec=pltpu.PrefetchScalarGridSpec(
            num_scalar_prefetch=1,
            grid=(parts,),
            in_specs=[
                first, first, second, second, some(0), some(0), some(index), full_block(4, features),
                full_block(features, width),
            ],
            out_specs=[
                some(0), full_block(chunk, features), full_block(8, features), full_block(8, features),
                full_block(chunk, width),
            ],
        ),
        compiler_params=pltpu.CompilerParams(vmem_limit_bytes=48 * 2**20),
        cost_estimate=SMALL,
        name="attention_low",
    )(middle, *came, between, attended, upstream, gains, weight)


def share_kernel(number, *rest):
    lefts, rights, (out_ref, turned_ref, right_ref, sems) = rest[:number], rest[number : 2 * number], rest[2 * number :]
    rows = lefts[0].shape[0]

    @pl.when(pl.program_id(0) == 0)
    def _():
        load_pieces(rights, right_ref, sems)

    for i, left in enumerate(lefts):
        turned_ref[:, i * rows : (i + 1) * rows] = left[...].T
    out = jnp.dot(turned_ref[...], right_ref[...], preferred_element_type=jnp.float32)
    out_ref[...] = out.astype(jnp.bfloat16)


def share_call(lefts, rights):
    number = len(rights)
    rows, columns = rights[0].shape
    features = lefts[0].shape[1]
    cut = len(lefts) == 1 and number > 1
    lefts = lefts * number if cut else lefts
    return pl.pallas_call(
        functools.partial(share_kernel, number),
        out_shape=jax.ShapeDtypeStruct((features, columns), jnp.bfloat16),
        grid=(features // TILE,),
        in_specs=[pl.BlockSpec((rows, TILE), lambda n, i=i * cut: (i, n)) for i in range(number)]
        + [pl.BlockSpec(memory_space=pl.ANY)] * number,
        out_specs=pl.BlockSpec((TILE, columns), lambda n: (n, 0)),
        scratch_shapes=[
            pltpu.VMEM((TILE, number * rows), jnp.bfloat16),
            pltpu.VMEM((number * rows, columns), jnp.bfloat16),
            pltpu.SemaphoreType.DMA((number,)),
        ],
        compiler_params=pltpu.CompilerParams(vmem_limit_bytes=48 * 2**20),
        cost_estimate=SMALL,
        name="share",
    )(*lefts, *rights)


def pair_sums_kernel(*refs):
    number = len(refs) // 3
    for i in range(number):
        left, right, out = refs[2 * i], refs[2 * i + 1], refs[2 * number + i]
        out[...] = (left[...].astype(jnp.float32) + right[...].astype(jnp.float32)).astype(jnp.bfloat16)


def pair_sums(pairs):
    rows, columns = pairs[0][0].shape
    tile = rows // 2
    block = pl.BlockSpec((tile, columns), lambda g: (g, 0))
    return pl.pallas_call(
        pair_sums_kernel,
        out_shape=[jax.ShapeDtypeStruct((rows, columns), jnp.bfloat16)] * len(pairs),
        grid=(rows // tile,),
        in_specs=[block] * (2 * len(pairs)),
        out_specs=[block] * len(pairs),
        compiler_params=pltpu.CompilerParams(vmem_limit_bytes=32 * 2**20),
        cost_estimate=SMALL,
        name="pair_sums",
    )(*[array for pair in pairs for array in pair])


def linear_back_kernel(query_grad_ref, group_ref, query_ref, weight_ref, hidden_ref, factor_ref, one_ref, two_ref, gain_ref):
    partial = lax.dot_general(query_grad_ref[...], query_ref[...], NT, preferred_element_type=jnp.float32)
    partial += lax.dot_general(group_ref[...], weight_ref[...], NT, preferred_element_type=jnp.float32)
    normed = hidden_ref[...].astype(jnp.float32) * factor_ref[:, :1]
    gain_ref[...] = fold(partial * normed)
    half = one_ref.shape[0]
    partial = partial.astype(jnp.bfloat16)
    one_ref[...] = partial[:half]
    two_ref[...] = partial[half:]


def linear_back(query_grad, query_block, group, group_block, query_weight, group_weight, hidden, factor, index, rows):
    features, width = query_weight.shape
    tile = WIDE
    row = pl.BlockSpec((rows, tile), lambda n: (index, n))
    weight = pl.BlockSpec((tile, width), lambda n: (n, 0))
    half = pl.BlockSpec((rows // 2, tile), lambda n: (0, n))
    return pl.pallas_call(
        linear_back_kernel,
        out_shape=(
            jax.ShapeDtypeStruct((rows // 2, features), jnp.bfloat16),
            jax.ShapeDtypeStruct((rows // 2, features), jnp.bfloat16),
            jax.ShapeDtypeStruct((8, features), jnp.float32),
        ),
        grid=(features // tile,),
        in_specs=[
            pl.BlockSpec((rows, width), lambda n: (query_block, 0)),
            pl.BlockSpec((rows, width), lambda n: (group_block, 0)),
            weight,
            weight,
            row,
            pl.BlockSpec((rows, 128), lambda n: (index, 0)),
        ],
        out_specs=[half, half, pl.BlockSpec((8, tile), lambda n: (0, n))],
        compiler_params=pltpu.CompilerParams(vmem_limit_bytes=32 * 2**20),
        cost_estimate=SMALL,
        name="linear_back",
    )(query_grad, group, query_weight, group_weight, hidden, factor)


def input_grad_kernel(middle_ref, *rest):
    came, (hidden_ref, upper_ref, gains_ref, *ignored, out_ref) = rest[:4], rest[4:]
    middle = middle_ref[0] == 1
    early = pl.program_id(0) < pl.num_programs(0) // 2
    rows = pl.ds(0, hidden_ref.shape[0])
    total = jnp.where(early, pick(middle, came[0], came[1], rows), pick(middle, came[2], came[3], rows))
    factor, normed = scaled(hidden_ref[...].astype(jnp.float32))
    raised = total * gains_ref[0:1, :]
    inner = jnp.mean(raised * normed, axis=-1, keepdims=True)
    out_ref[...] = upper_ref[...] + factor * (raised - normed * inner)


def input_grad(middle, came, hidden, upper, upper_block, gains, index, before):
    half, features = came[0].shape
    size = min(ROW, half)
    parts = 2 * half // size

    def some(block):
        return pl.BlockSpec((size, features), lambda n, m: (block * parts + n, 0))

    first = pl.BlockSpec((size, features), lambda n, m: (jnp.minimum(n, parts // 2 - 1), 0))
    second = pl.BlockSpec((size, features), lambda n, m: (jnp.maximum(n - parts // 2, 0), 0))
    extra = [] if before is None else [before]
    return pl.pallas_call(
        input_grad_kernel,
        out_shape=jax.ShapeDtypeStruct(hidden.shape, jnp.float32),
        grid_spec=pltpu.PrefetchScalarGridSpec(
            num_scalar_prefetch=1,
            grid=(parts,),
            in_specs=[first, first, second, second, some(index), some(upper_block), full_block(4, features)]
            + [pl.BlockSpec(memory_space=pl.ANY)] * len(extra),
            out_specs=some(index),
        ),
        input_output_aliases={8: 0} if extra else {},
        compiler_params=pltpu.CompilerParams(vmem_limit_bytes=32 * 2**20),
        cost_estimate=SMALL,
        name="input_grad",
    )(middle, *came, hidden, upper, gains, *extra)


THETA = 10000.0
ROWS = ("dp", "seq")
LINE = "tensor"
LOW = jnp.bfloat16
FULL = jnp.float32
CHUNK = 512
FINE = 256
BUDGET = 48.0
FINE_BUDGET = 30.0
(HEADS, STAT, ATTENDED, BETWEEN, NORMED, GATE, UP, MIXED, FED, RESULT, FED_LOW, GAIN_ONE, GAIN_TWO, GAIN_THREE,
 GAIN_FOUR, GATE_LOW, UP_LOW, NORMED_GRAD, MIDDLE_GRAD, ATTENTION_LOW, QUERY_GRAD, SUMS, SPREAD, GROUP,
 LINEAR, INPUT_GRAD, SHARE, BESIDE, PASSED, BELOW, TOTAL) = range(31)
DOWN_SHARE, GATE_SHARE, UP_SHARE, LINEAR_SHARE = range(4)


def dot(a, b, dims=(((1,), (0,)), ((), ()))):
    return lax.dot_general(a, b, dims, preferred_element_type=FULL)


def angles(places, width):
    half = width // 2
    frequency = jnp.power(THETA, -2.0 * jnp.arange(half, dtype=FULL) / width)
    turned = places.astype(FULL)[:, None] * frequency[None, :]
    return (jnp.cos(turned), jnp.sin(turned))


def gather(weight):
    return lax.all_gather(weight, ROWS, axis=0, tiled=True)


def scatter(grad):
    return lax.psum_scatter(grad, ROWS, scatter_dimension=0, tiled=True)


def hop_by(array, hop, seqs):
    return lax.ppermute(array, "seq", [(i, i + hop) for i in range(seqs - hop)])


def hop_back(array, hop, seqs):
    return lax.ppermute(array, "seq", [(i + hop, i) for i in range(seqs - hop)])


def cut(array, pieces):
    size = array.shape[0] // pieces
    return [array[i * size : (i + 1) * size] for i in range(pieces)]


def fetch_window(own, reach, seqs, later):
    if seqs != 4 or reach != 2:
        return [hop_by(own, hop, seqs) for hop in range(reach, 0, -1)]
    near, far = [], []
    last = lax.axis_index("seq") == 2
    pieces = cut(own, 4)
    pieces[3] = lax.optimization_barrier((pieces[3], later()))[0]
    for piece in pieces:
        beside = lax.ppermute(piece, "seq", [(0, 1), (2, 3)])
        below = lax.ppermute(piece, "seq", [(0, 2), (1, 3)])
        passed = lax.ppermute(below, "seq", [(3, 2)])
        near.append((beside, passed))
        far.append(below)
    return [far, [jnp.where(last, passed, beside) for beside, passed in near]]


class Schedule:
    def __init__(self, token, count):
        self.count = count
        self.token = token
        self.values = {}
        self.ready = {}
        self.jobs = []
        self.lines = [[], []]
        self.entered = []
        self.stages = [[None, None, None], [None, None, None]]
        self.now = 0
        self.late = []

    def job(self, cost, needs, work):
        self.jobs.append((cost, needs, work))

    def enter(self, name, halves):
        self.entered.append((name, halves))

    def after(self, *arrays):
        return lax.optimization_barrier((arrays, self.token))[0]

    def barrier(self, *arrays):
        self.token, arrays = lax.optimization_barrier((self.token, arrays))
        return arrays

    def move(self, half, arrived):
        inward, across, outward = (
            None if item is None else (item[0],) + tuple(two) for item, two in zip(self.stages[half], arrived)
        )
        moved = [None, None, None]
        if self.lines[half]:
            name, part = self.lines[half].pop(0)
            moved[0] = (name, part, lax.ppermute(part, LINE, [(0, 1), (3, 2)]))
        pairs = [item[1:] for item in (inward, across) if item is not None]
        sums = list(pair_sums(pairs)) if pairs and pairs[0][0].shape == pairs[-1][0].shape else [
            pair_sums([pair])[0] for pair in pairs]
        if inward is not None:
            pair = sums.pop(0)
            moved[1] = (inward[0], pair, lax.ppermute(pair, LINE, [(1, 2), (2, 1)]))
        if across is not None:
            total = sums.pop(0)
            moved[2] = (across[0], total, lax.ppermute(total, LINE, [(1, 0), (2, 3)]))
        self.stages[half] = moved
        return outward

    def tick(self, budget):
        made, spent, left = {}, 0.0, []
        for cost, needs, work in self.jobs:
            fits = spent == 0.0 or spent + cost <= budget
            if fits and all(self.ready.get(need, self.now + 1) <= self.now for need in needs):
                made.update(work())
                spent += cost
            else:
                left.append((cost, needs, work))
        self.jobs = left
        late = [item for item in self.late if item[1] <= self.now]
        self.late = [item for item in self.late if item[1] > self.now]
        entered, self.entered = self.entered, []
        waiting = [[None if item is None else item[1:] for item in stages] for stages in self.stages]
        made, halves, brought, first = self.barrier(
            made, [item[1] for item in entered], [item[2] for item in late], waiting[0]
        )
        for (name, ignored), (one, two) in zip(entered, halves):
            self.lines[0].append((name, one))
            self.lines[1].append((name, two))
        one = self.move(0, first)
        (second,) = self.barrier(waiting[1])
        two = self.move(1, second)
        if one is not None:
            made[one[0]] = one[1:] + two[1:]
        for item, value in zip(late, brought):
            made[item[0]] = value
        self.now += 1
        for name, value in made.items():
            self.values[name] = value
            self.ready[name] = self.now

    def run(self):
        while self.jobs or self.late or any(self.lines) or any(any(stages) for stages in self.stages):
            self.tick(FINE_BUDGET if self.ready.get((SUMS, self.count), self.now + 1) <= self.now else BUDGET)


def per_device(
    inputs,
    positions,
    query_weight,
    key_weight,
    value_weight,
    output_weight,
    gate_weight,
    up_weight,
    down_weight,
    pre_attention,
    post_attention,
    pre_feedforward,
    post_feedforward,
    cotangent,
):
    hidden = inputs[0]
    upstream = cotangent[0]
    places = positions[0]
    rows, features = hidden.shape
    chunk = min(CHUNK, rows)
    count = rows // chunk
    fine = min(FINE, chunk)
    fines = rows // fine
    split = chunk // fine
    seqs = lax.axis_size("seq")
    reach = min((WINDOW + rows - 2) // rows, seqs - 1)
    heads_width = query_weight.shape[1]
    group_width = key_weight.shape[1]

    gains = jnp.stack([pre_attention, post_attention, pre_feedforward, post_feedforward], axis=1)
    gains = jnp.pad(gains, ((0, 0), (0, 124)))
    packed = gather(jnp.concatenate([key_weight, value_weight, gains], axis=1))
    group_full = packed[:, : 2 * group_width]
    gains = 1.0 + packed[:, 2 * group_width : 2 * group_width + 4].astype(FULL).T
    query_weight, output_weight, packed = lax.optimization_barrier((query_weight, output_weight, packed))
    query_full = gather(query_weight)
    output_full = gather(output_weight)

    cosine, sine = angles(places, HD)
    normed_one, own, factor = project_group(hidden, gains[:1], group_full, cosine, sine)
    query_low = project_heads(normed_one, query_full, cosine, sine)
    fetched = fetch_window(own, reach, seqs, lambda: query_low)
    low, bounds = limits(places, chunk)
    low_wide = jnp.broadcast_to(low[:, None], (rows, 128))
    low_row = low[None, :]
    fetched, query_low, low_wide, low_row, bounds, gate_weight, up_weight, down_weight = lax.optimization_barrier(
        (fetched, query_low, low_wide, low_row, bounds, gate_weight, up_weight, down_weight)
    )
    blocks = []
    for block in fetched:
        blocks += block if isinstance(block, list) else [block]
    blocks += cut(own, rows // blocks[0].shape[0])
    gate_full = gather(gate_weight)
    up_full = gather(up_weight)
    down_full = gather(down_weight)

    place = lax.axis_index(LINE)
    middle = ((place == 1) | (place == 2)).astype(jnp.int32)[None]
    plan = Schedule(bounds[0, 0], count)
    values = plan.values

    def part(array, index, size=chunk):
        return array[index * size : (index + 1) * size]

    def every(kind, number):
        return [values[kind, i] for i in range(number)]

    def attend_job(i):
        def work():
            (query,) = plan.after(query_low)
            head, stat = attend(query, blocks, low_wide, bounds, i, 1, chunk)
            plan.enter((ATTENDED, i), back_out([(head, output_full)], chunk // 2))
            return {(HEADS, i): head, (STAT, i): stat}

        plan.job(12.0 if i else 40.0, [], work)

    def forward_job(i):
        def work():
            kinds = (ATTENDED, BETWEEN, NORMED, GATE, UP, MIXED)
            made = gate_call(middle, values[ATTENDED, i], hidden, gains, gate_full, up_full, i)
            plan.enter((FED, i), back_out([(made[5], down_full)], chunk // 2))
            return {(kind, i): array for kind, array in zip(kinds, made)}

        plan.job(36.0, [(ATTENDED, i)], work)

    def backward_job(i):
        def work():
            kinds = (RESULT, FED_LOW, GAIN_FOUR, GATE_LOW, UP_LOW)
            made = mixed_back(
                middle, values[FED, i], values[BETWEEN, i], upstream, gains, down_full,
                values[GATE, i], values[UP, i], i, values.get((RESULT, 0)),
            )
            values[RESULT, 0] = made[0]
            plan.enter((NORMED_GRAD, i), back_out([(made[3], gate_full), (made[4], up_full)], chunk // 2))
            return {(kind, i): array for kind, array in zip(kinds[1:], made[1:])}

        plan.job(40.0, [(FED, i)], work)

    def attention_job(i):
        def work():
            kinds = (MIDDLE_GRAD, ATTENTION_LOW, GAIN_TWO, GAIN_THREE)
            *made, heads_grad = attention_low(
                middle, values[NORMED_GRAD, i], values[BETWEEN, i], values[ATTENDED, i], upstream, gains, output_full, i
            )
            query_grad, *sums = attend_back(
                query_low, heads_grad, values[HEADS, i], values[STAT, i], blocks, low_row,
                cosine, sine, bounds, values.get((SUMS, i)), i, 1, chunk, sent if i == count - 1 else (),
            )
            made = {(kind, i): array for kind, array in zip(kinds, made)}
            made.update({(QUERY_GRAD, i): query_grad, (SUMS, i + 1): sums[-1]})
            made.update({(SPREAD, k): array for k, array in enumerate(sums[:-1])})
            return made

        plan.job(44.0, [(NORMED_GRAD, i)] + ([(SUMS, i)] if i else []), work)

    def first_spread_job():
        def work():
            for k in range(4):
                near = values[SPREAD, 4 + k]
                beside = lax.ppermute(near, "seq", [(1, 0), (3, 2)])
                passed = lax.ppermute(near, "seq", [(2, 3)])
                plan.late.append(((BESIDE, k), plan.now + k // 2 + 1, beside))
                plan.late.append(((PASSED, k), plan.now + k // 2, passed))
            return {}

        plan.job(1.0, [(SUMS, count)], work)

    def second_spread_job(k):
        def work():
            (below,) = pair_sums([(values[SPREAD, k], values[PASSED, k])])
            plan.late.append(((BELOW, k), plan.now, lax.ppermute(below, "seq", [(2, 0), (3, 1)])))
            return {}

        plan.job(1.0, [(PASSED, k)], work)

    def hops_job():
        def work():
            for hop in range(1, reach + 1):
                plan.late.append(((BESIDE, hop), plan.now + 1, hop_back(values[SPREAD, reach - hop], hop, seqs)))
            return {}

        plan.job(1.0, [(SUMS, count)], work)

    def group_job(k, needs):
        def work():
            arrived = [values[need] for need in needs]
            group = finish_group(values[SUMS, count], arrived, cosine, sine, k)
            made = {(GROUP, k): group}
            each = fines // groups
            for i in range(k * each, (k + 1) * each):
                *halves, made[GAIN_ONE, i] = linear_back(
                    values[QUERY_GRAD, i // split], i % split, group, i - k * each, query_full, group_full,
                    hidden, factor, i, fine,
                )
                plan.enter((LINEAR, i), halves)
            return made

        plan.job(3.0 + 5.0 * fines // groups, needs, work)

    def input_job(i):
        def work():
            return {(INPUT_GRAD, i + 1): input_grad(
                middle, values[LINEAR, i], hidden, values[MIDDLE_GRAD, i // split], i % split, gains, i,
                values.get((INPUT_GRAD, i)),
            )}

        plan.job(4.0, [(LINEAR, i)] + [(INPUT_GRAD, i)] * (i > 0), work)

    def share_job(index, cost, needs, left, right):
        def work():
            lefts = left()
            lefts[0], = plan.after(lefts[0])
            return {(SHARE, index): share_call(lefts, right())}

        plan.job(cost, needs, work)

    def scatter_job(index, ticks, needs):
        def work():
            (share,) = plan.after(values[SHARE, index])
            plan.late.append(((TOTAL, index), plan.now + ticks - 1, scatter(share)))
            return {}

        plan.job(0.0, [(SHARE, index)] + needs, work)

    def linear_share_job():
        def work():
            kinds = ((GAIN_ONE, fines), (GAIN_TWO, count), (GAIN_THREE, count), (GAIN_FOUR, count))
            columns = jnp.stack([jnp.sum(sum(every(*kind)), axis=0) for kind in kinds], axis=1)
            columns = jnp.pad(columns.astype(LOW), ((0, 0), (0, 124)))
            (left,) = plan.after(normed_one)
            grads = [share_call([left], every(QUERY_GRAD, count)), share_call([left], every(GROUP, groups))]
            grads.append(share_call(every(ATTENTION_LOW, count), every(HEADS, count)))
            return {(SHARE, LINEAR_SHARE): jnp.concatenate(grads + [columns], axis=1)}

        plan.job(30.0, [(GAIN_ONE, i) for i in range(fines)], work)

    square = seqs == 4 and reach == 2
    groups = 4 if square else 1
    sent = (rows // 4,) * 8 if square else (rows,) * reach
    for i in range(count):
        attend_job(i)
    for i in range(count):
        forward_job(i)
    for i in range(count):
        backward_job(i)
    for i in range(count):
        attention_job(i)
    if square:
        first_spread_job()
        for k in range(4):
            second_spread_job(k)
        for k in range(4):
            group_job(k, [(BESIDE, k), (BELOW, k)])
    else:
        hops_job()
        group_job(0, [(BESIDE, hop) for hop in range(1, reach + 1)])
    backs = [(GATE_LOW, i) for i in range(count)] + [(SUMS, count)]
    share_job(DOWN_SHARE, 26.0, backs, lambda: every(FED_LOW, count), lambda: every(MIXED, count))
    share_job(GATE_SHARE, 26.0, backs, lambda: every(NORMED, count), lambda: every(GATE_LOW, count))
    share_job(UP_SHARE, 26.0, backs, lambda: every(NORMED, count), lambda: every(UP_LOW, count))
    linear_share_job()
    scatter_job(DOWN_SHARE, 2, [(GROUP, 0)] if groups == 1 else [(BELOW, 1)])
    scatter_job(GATE_SHARE, 2, [(TOTAL, DOWN_SHARE)])
    scatter_job(UP_SHARE, 3, [(TOTAL, GATE_SHARE)])
    scatter_job(LINEAR_SHARE, 2, [(TOTAL, UP_SHARE)])
    for i in range(fines):
        input_job(i)
    plan.run()

    shares = [array.astype(FULL) for array in every(TOTAL, 4)]
    linear_share = shares[LINEAR_SHARE]
    width = heads_width + 2 * group_width
    gain_grads = linear_share[:, width + heads_width :][:, :4].T
    gain_one = gain_grads[0]
    for turn in (1, 2):
        gain_one = gain_one + lax.ppermute(gain_one, LINE, [(i, i ^ turn) for i in range(4)])
    return (
        values[RESULT, 0][None],
        values[INPUT_GRAD, fines][None],
        linear_share[:, :heads_width],
        linear_share[:, heads_width : heads_width + group_width],
        linear_share[:, heads_width + group_width : width],
        linear_share[:, width : width + heads_width],
        shares[GATE_SHARE],
        shares[UP_SHARE],
        shares[DOWN_SHARE],
        gain_one,
        gain_grads[1],
        gain_grads[2],
        gain_grads[3],
    )


def solution(mesh):
    tokens = P("dp", "seq", None)
    weight = P(ROWS, LINE)
    gain = P(ROWS)
    return jax.shard_map(
        per_device,
        mesh=mesh,
        in_specs=(tokens, P("dp", "seq")) + (weight,) * 7 + (gain,) * 4 + (tokens,),
        out_specs=(tokens, tokens) + (weight,) * 7 + (gain,) * 4,
        check_vma=False,
    )
```
